128 devices in a mesh: pair: 8 (over y, core), row: 16 (over z, x).
Axes of the slice: x: 4, y: 4, z: 4, core: 2. Of those that a mesh axis runs over, the one named last changes fastest.
Arguments:
- matrix: float32 [8192, 8192], P('row', 'pair'), may hold values from -12 to 12
- sources: int32 [3, 32], replicated, may hold values from 0 to 31, as said below
Outputs:
- rotated_matrix: float32 [8192, 8192], P('row', 'pair')
The draws below stay inside these ranges and needn't reach their ends.
Inputs may be any that keep to these rules, and one draw needn't show every extreme that they name: `sources`: each round's row is a permutation of the slots. A slot's source lies on its own index of pair or on the next lower or higher one (slots per index: 4); for each index at most one slot draws from the lower neighbour and at most one from the higher one, with no wrap.
All inputs are finite; a program needn't handle non-finite values.
Results may differ from the reference program's by a relative error of at most 0.00016.
Values sent between devices are 32-bit elements; how exact they have to be, the bound alone decides.
No kernel may reach another device: no remote copies, remote signals or barrier semaphores. Data moves between devices by JAX's collectives and lax.ppermute only.
A program may use at most 320 MiB of HBM per device.

```python
from functools import partial
import jax
import jax.numpy as jnp
from jax import lax

BLOCK = 256
ROUNDS = 3
NS_ITERS = 3
NBLOCKS = 32
COLS = 8192
ROWS = 8192


def draw_sources(key, part):
    key = jax.random.fold_in(key, 11)
    pair_total = NBLOCKS // 2
    slot_ids = jnp.arange(NBLOCKS, dtype=jnp.int32)
    pair_ids = slot_ids // 2
    role_ids = slot_ids % 2
    top_source = jnp.where(pair_ids == 0, 0, jnp.where(pair_ids == 1, 1, 2 * (pair_ids - 1)))
    bottom_source = jnp.where(pair_ids == pair_total - 1, 2 * (pair_total - 1), 2 * (pair_ids + 1) + 1)
    forward = jnp.where(role_ids == 0, top_source, bottom_source).astype(jnp.int32)
    mirror = (2 * (pair_total - 1 - pair_ids) + role_ids).astype(jnp.int32)
    backward = mirror[forward[mirror]]
    key_dir, key_swap = jax.random.split(key)
    directions = jax.random.randint(key_dir, (ROUNDS,), 0, 2)
    swaps = jax.random.randint(key_swap, (ROUNDS, pair_total), 0, 2).astype(jnp.int32)
    base_table = jnp.where(directions[:, None] == 1, backward[None, :], forward[None, :])
    flips = swaps[:, pair_ids]
    picked = jnp.bitwise_xor(slot_ids[None, :], flips)
    return jnp.take_along_axis(base_table, picked, axis=1).astype(jnp.int32)


def shard_levels(rng, dims, cuts, smallest, top_value):
    gain, own = 1.0, jax.random.fold_in(rng, 6)
    for axis_at, shards_of in cuts:
        heights = jnp.exp(jax.random.uniform(jax.random.fold_in(own, axis_at), (shards_of,), jnp.float32, smallest / len(cuts), top_value / len(cuts)))
        gain = gain * jnp.repeat(heights, dims[axis_at] // shards_of).reshape([-1 if axis == axis_at else 1 for axis in range(len(dims))])
    return gain


def gaussian(key, dims, scale, most, shards=(), kind=jnp.bfloat16):
    drawn = scale * jax.random.normal(key, dims, jnp.float32)
    if shards:
        drawn = drawn * shard_levels(key, dims, shards, -0.22, 0.18)
    return jnp.clip(drawn, -most, most).astype(kind)


def setup_inputs(seed: int = 0) -> dict:
    splits = jax.random.split(jax.random.key(seed), 3)
    matrix = gaussian(splits[0], (ROWS, COLS), 2.0, 12.0, ((0, 16), (1, 8)), jnp.float32)
    sources = draw_sources(jax.random.fold_in(splits[2], 71), 0)
    return {"matrix": matrix, "sources": sources}


HIGHEST = lax.Precision.HIGHEST

def rotation(gram_matrix, row_count):
    scaled = gram_matrix / row_count
    inverse_root = lax.rsqrt(jnp.diagonal(scaled) + 1e-06)
    correlation = scaled * inverse_root[:, None] * inverse_root[None, :]
    generator = jnp.triu(correlation, 1) - jnp.tril(correlation, -1)
    spread = jnp.sqrt(jnp.sum(generator * generator))
    identity = jnp.eye(gram_matrix.shape[0], dtype=jnp.float32)
    iterate = (identity - generator) / (1.0 + spread)
    for sweep in range(NS_ITERS):
        product = jnp.dot(iterate.T, iterate, precision=HIGHEST)
        iterate = 1.5 * iterate - 0.5 * jnp.dot(iterate, product, precision=HIGHEST)
    return iterate

def reference(matrix, sources):
    current = matrix
    pair_total = NBLOCKS // 2
    for round_index in range(ROUNDS):
        pair_view = current.reshape(ROWS, pair_total, 2 * BLOCK)
        pair_grams = jnp.einsum('mpi,mpj->pij', pair_view, pair_view, precision=HIGHEST)
        rotations = jax.vmap(partial(rotation, row_count=ROWS))(pair_grams)
        pair_view = jnp.einsum('mpi,pij->mpj', pair_view, rotations, precision=HIGHEST)
        block_view = pair_view.reshape(ROWS, NBLOCKS, BLOCK)
        current = jnp.take(block_view, sources[round_index], axis=1).reshape(ROWS, COLS)
    return current
```

```python
from functools import partial

import jax
import jax.numpy as jnp
from jax import lax
from jax.experimental import pallas as pl
from jax.experimental.pallas import tpu as pltpu
from jax.sharding import PartitionSpec as P

BLOCK = 256
PAIR = 2 * BLOCK
ROUNDS = 3
F32 = jnp.float32
BF16 = jnp.bfloat16
POLY = (2.25, -2.4375, 1.6875, -0.5625, 0.0625)

VMEM = pl.BlockSpec(memory_space=pltpu.VMEM)
SMEM = pl.BlockSpec(memory_space=pltpu.SMEM)
PARAMS = pltpu.CompilerParams(vmem_limit_bytes=56 * 1024 * 1024)


def call(kernel, out_shape, in_specs, scratch=(), flops=0):
    return pl.pallas_call(
        kernel,
        out_shape=out_shape,
        in_specs=in_specs,
        out_specs=jax.tree.map(lambda _: VMEM, out_shape),
        scratch_shapes=list(scratch),
        compiler_params=PARAMS,
        cost_estimate=pl.CostEstimate(flops=flops, bytes_accessed=4_000_000, transcendentals=0),
    )


def split(x):
    high = x.astype(BF16)
    return high, (x - high.astype(F32)).astype(BF16)


def dot(a, b):
    return jnp.dot(a, b, preferred_element_type=F32)


def dot_t(a, b):
    return lax.dot_general(a, b, (((0,), (0,)), ((), ())), preferred_element_type=F32)


def product(ah, al, bh, bl, cols, mul=dot):
    return mul(ah[...], bh[:, cols]) + (mul(ah[...], bl[:, cols]) + mul(al[...], bh[:, cols]))


def eye_mask(n):
    return lax.broadcasted_iota(jnp.int32, (n, n), 0) == lax.broadcasted_iota(jnp.int32, (n, n), 1)


def upper_mask(n):
    return lax.broadcasted_iota(jnp.int32, (n, n), 0) < lax.broadcasted_iota(jnp.int32, (n, n), 1)


def own_source(src_ref, dev_ref, round_index, slot, slots):
    base = dev_ref[0] * slots
    return src_ref[round_index, base + slot] - base


def leaving(src_ref, dev_ref, round_index, step, slots):
    base = dev_ref[0] * slots
    last = src_ref.shape[1] - slots
    there = jnp.clip(base + step * slots, 0, last)
    found = jnp.int32(0)
    for slot in range(slots):
        offset = src_ref[round_index, there + slot] - base
        found = jnp.where((offset >= 0) & (offset < slots), offset, found)
    return found


def picked(offset, slots, own_ref, lower_ref, upper_ref):
    own = own_ref[jnp.clip(offset, 0, slots - 1)]
    return jnp.where(offset < 0, lower_ref[...], jnp.where(offset >= slots, upper_ref[...], own))


def first_gram(a_ref, part_ref, high_ref, low_ref):
    pairs = a_ref.shape[1] // PAIR
    chunks = part_ref.shape[0]
    rows = part_ref.shape[1] - 8
    per = BLOCK // rows
    part_ref[:, rows:, :] = jnp.zeros((chunks, 8, BLOCK), F32)
    high, low = split(a_ref[...])
    high_ref[...] = high
    low_ref[...] = low
    for p in range(pairs):
        one, two = pl.ds(p * PAIR, BLOCK), pl.ds(p * PAIR + BLOCK, BLOCK)

        def gram(x, y):
            return dot_t(high_ref[:, x], high_ref[:, y]) + (
                dot_t(high_ref[:, x], low_ref[:, y]) + dot_t(low_ref[:, x], high_ref[:, y])
            )

        cross = gram(one, two)
        first = gram(one, one)
        second = gram(two, two)
        eye = eye_mask(BLOCK)
        diagonal = jnp.sum(jnp.where(eye, second, 0.0), axis=0, keepdims=True)
        both = jnp.where(eye | upper_mask(BLOCK), first, second)
        start = 2 * per * p
        for j in range(per):
            part_ref[start + j, :rows, :] = cross[j * rows:(j + 1) * rows]
            part_ref[start + per + j, :rows, :] = both[j * rows:(j + 1) * rows]
        part_ref[start, rows:, :] = jnp.broadcast_to(diagonal, (8, BLOCK))


def cross_gram(round_index, slots, src_ref, dev_ref, own_ref, lower_ref, upper_ref, part_ref, high_ref, low_ref):
    rows = part_ref.shape[1]
    per = BLOCK // rows
    for slot in range(slots):
        offset = own_source(src_ref, dev_ref, round_index, slot, slots)
        high, low = split(picked(offset, slots, own_ref, lower_ref, upper_ref))
        high_ref[:, pl.ds(slot * BLOCK, BLOCK)] = high
        low_ref[:, pl.ds(slot * BLOCK, BLOCK)] = low
    for p in range(slots // 2):
        one, two = pl.ds(p * PAIR, BLOCK), pl.ds(p * PAIR + BLOCK, BLOCK)
        cross = dot_t(high_ref[:, one], high_ref[:, two]) + (
            dot_t(high_ref[:, one], low_ref[:, two]) + dot_t(low_ref[:, one], high_ref[:, two])
        )
        for j in range(per):
            part_ref[p * per + j] = cross[j * rows:(j + 1) * rows]


def set_generator(total_rows, cross, first, second, kf, kh, kl):
    eye = eye_mask(BLOCK)
    sign = jnp.where(eye, 0.0, jnp.where(upper_mask(BLOCK), 1.0, -1.0))
    scale = 1.0 / total_rows
    roots = []
    for block in (first, second):
        kept = jnp.where(eye, block * scale, 0.0)
        roots.append(
            (
                lax.rsqrt(jnp.sum(kept, axis=1, keepdims=True) + 1e-06),
                lax.rsqrt(jnp.sum(kept, axis=0, keepdims=True) + 1e-06),
            )
        )
    k11 = first * scale * roots[0][0] * roots[0][1] * sign
    k22 = second * scale * roots[1][0] * roots[1][1] * sign
    k12 = cross * scale * roots[0][0] * roots[1][1]
    total = jnp.sum(k11 * k11 + k22 * k22 + 2.0 * (k12 * k12), keepdims=True)
    lo, hi = pl.ds(0, BLOCK), pl.ds(BLOCK, BLOCK)
    for r, c, block in ((lo, lo, k11), (lo, hi, k12), (hi, lo, -k12.T), (hi, hi, k22)):
        kf[r, c] = block
        high, low = split(block)
        kh[r, c] = high
        kl[r, c] = low
    return 1.0 / (1.0 + jnp.sqrt(total))


def rotations(scales, work, out_high, out_low):
    pairs = len(scales)
    halves = [pl.ds(0, BLOCK), pl.ds(BLOCK, BLOCK)]
    both = [(p, cols) for p in range(pairs) for cols in halves]
    coefficients = []
    for c in scales:
        u = c * c
        b0, b1, b2, b3, b4 = POLY
        coefficients.append(
            (
                u,
                b0 + u * (b1 + u * (b2 + u * (b3 + u * b4))),
                b1 + u * (2 * b2 + u * (3 * b3 + u * 4 * b4)),
                b2 + u * (3 * b3 + u * 6 * b4),
                b3 + u * 4 * b4,
                b4,
            )
        )
    for p, cols in both:
        kf, kh, kl, sf, sh, sl, vf, vh, vl, th, tl, xh, xl, yh, yl = work[p]
        s = -coefficients[p][0] * product(kh, kl, kh, kl, cols)
        sf[:, cols] = s
        sh[:, cols], sl[:, cols] = split(s)
    for p, cols in both:
        kf, kh, kl, sf, sh, sl, vf, vh, vl, th, tl, xh, xl, yh, yl = work[p]
        u, a0, a1, a2, a3, a4 = coefficients[p]
        v = product(sh, sl, sh, sl, cols)
        vf[:, cols] = v
        vh[:, cols], vl[:, cols] = split(v)
        th[:, cols], tl[:, cols] = split(a3 * sf[:, cols] + a4 * v)
    for p, cols in both:
        kf, kh, kl, sf, sh, sl, vf, vh, vl, th, tl, xh, xl, yh, yl = work[p]
        u, a0, a1, a2, a3, a4 = coefficients[p]
        t = a1 * sf[:, cols] + a2 * vf[:, cols] + product(vh, vl, th, tl, cols)
        vf[:, cols] = t
        sh[:, cols], sl[:, cols] = split(t)
    for p, cols in both:
        kf, kh, kl, sf, sh, sl, vf, vh, vl, th, tl, xh, xl, yh, yl = work[p]
        u, a0, a1, a2, a3, a4 = coefficients[p]
        c = scales[p]
        odd = a0 * kf[:, cols] + product(kh, kl, sh, sl, cols)
        row = lax.broadcasted_iota(jnp.int32, (PAIR, BLOCK), 0)
        col = lax.broadcasted_iota(jnp.int32, (PAIR, BLOCK), 1) + cols.start
        even = jnp.where(row == col, vf[:, cols] + a0, vf[:, cols])
        x = c * (even - odd)
        sf[:, cols] = x
        xh[:, cols], xl[:, cols] = split(x)
        yh[:, cols], yl[:, cols] = split(c * (even + odd))
    for p, cols in both:
        kf, kh, kl, sf, sh, sl, vf, vh, vl, th, tl, xh, xl, yh, yl = work[p]
        vh[:, cols], vl[:, cols] = split(product(yh, yl, xh, xl, cols))
    for p, cols in both:
        kf, kh, kl, sf, sh, sl, vf, vh, vl, th, tl, xh, xl, yh, yl = work[p]
        r = 1.5 * sf[:, cols] - 0.5 * product(xh, xl, vh, vl, cols)
        out_high[p, :, cols], out_low[p, :, cols] = split(r)


def apply(round_index, slots, src_ref, dev_ref, high_ref, low_ref, rh_ref, rl_ref, own_ref, right_ref, left_ref):
    for p in range(slots // 2):
        ah, al = high_ref.at[:, pl.ds(p * PAIR, PAIR)], low_ref.at[:, pl.ds(p * PAIR, PAIR)]
        for half in range(2):
            own_ref[2 * p + half] = product(ah, al, rh_ref.at[p], rl_ref.at[p], pl.ds(half * BLOCK, BLOCK))
    right_ref[...] = own_ref[leaving(src_ref, dev_ref, round_index, 1, slots)]
    left_ref[...] = own_ref[leaving(src_ref, dev_ref, round_index, -1, slots)]


def first_rotate(total_rows, slots, src_ref, dev_ref, sum_ref, high_ref, low_ref,
                 own_ref, right_ref, left_ref, rh_ref, rl_ref, gh_ref, gl_ref, *work):
    rows = sum_ref.shape[1] - 8
    per = BLOCK // rows
    work = [work[15 * p:15 * p + 15] for p in range(slots // 2)]
    scales = []
    lo, hi = pl.ds(0, BLOCK), pl.ds(BLOCK, BLOCK)
    for p in range(slots // 2):
        start = 2 * per * p
        cross = sum_ref[start:start + per, :rows, :].reshape(BLOCK, BLOCK)
        both = sum_ref[start + per:start + 2 * per, :rows, :].reshape(BLOCK, BLOCK)
        diagonal = sum_ref[start, rows:rows + 1, :]
        turned = both.T
        eye, upper = eye_mask(BLOCK), upper_mask(BLOCK)
        first = jnp.where(eye | upper, both, turned)
        second = jnp.where(eye, diagonal, jnp.where(upper, turned, both))
        for r, c, block in ((lo, lo, first), (lo, hi, cross), (hi, lo, cross.T), (hi, hi, second)):
            high, low = split(block)
            gh_ref[p, r, c] = high
            gl_ref[p, r, c] = low
        scales.append(set_generator(total_rows, cross, first, second, *work[p][:3]))
    rotations(scales, work, rh_ref, rl_ref)
    apply(0, slots, src_ref, dev_ref, high_ref, low_ref, rh_ref, rl_ref, own_ref, right_ref, left_ref)


def later_rotate(round_index, last, total_rows, slots, src_ref, dev_ref, sum_ref, self_ref, lower_ref, upper_ref,
                 high_ref, low_ref, own_ref, right_ref, left_ref, rh_ref, rl_ref, gh_ref, gl_ref, *work):
    rows = sum_ref.shape[1]
    per = BLOCK // rows
    work = [work[15 * p:15 * p + 15] for p in range(slots // 2)]
    scales = []
    lo, hi = pl.ds(0, BLOCK), pl.ds(BLOCK, BLOCK)
    for p in range(slots // 2):
        cross = sum_ref[p * per:p * per + per].reshape(BLOCK, BLOCK)
        first, second = (
            picked(own_source(src_ref, dev_ref, round_index - 1, 2 * p + half, slots), slots, self_ref, lower_ref, upper_ref)
            for half in range(2)
        )
        if not last:
            for r, c, block in ((lo, lo, first), (lo, hi, cross), (hi, lo, cross.T), (hi, hi, second)):
                high, low = split(block)
                gh_ref[p, r, c] = high
                gl_ref[p, r, c] = low
        scales.append(set_generator(total_rows, cross, first, second, *work[p][:3]))
    rotations(scales, work, rh_ref, rl_ref)
    apply(round_index, slots, src_ref, dev_ref, high_ref, low_ref, rh_ref, rl_ref, own_ref, right_ref, left_ref)


def carry_self(round_index, slots, src_ref, dev_ref, gh_ref, gl_ref, rh_ref, rl_ref,
               self_ref, right_ref, left_ref, yh, yl):
    for p in range(slots // 2):
        for half in range(2):
            cols = pl.ds(half * BLOCK, BLOCK)
            yh[...], yl[...] = split(product(gh_ref.at[p], gl_ref.at[p], rh_ref.at[p], rl_ref.at[p], cols))
            self_ref[2 * p + half] = dot_t(rh_ref[p, :, cols], yh[...]) + (
                dot_t(rh_ref[p, :, cols], yl[...]) + dot_t(rl_ref[p, :, cols], yh[...])
            )
    right_ref[...] = self_ref[leaving(src_ref, dev_ref, round_index, 1, slots)]
    left_ref[...] = self_ref[leaving(src_ref, dev_ref, round_index, -1, slots)]


def settle(round_index, slots, src_ref, dev_ref, own_ref, lower_ref, upper_ref, out_ref):
    for slot in range(slots):
        offset = own_source(src_ref, dev_ref, round_index, slot, slots)
        out_ref[:, pl.ds(slot * BLOCK, BLOCK)] = picked(offset, slots, own_ref, lower_ref, upper_ref)


def to_next(x, by):
    count = lax.axis_size("pair")
    return lax.ppermute(x, "pair", [(i, i + by) for i in range(count) if 0 <= i + by < count])


def sum_rows(part):
    pieces = lax.all_to_all(part, "row", 0, 0, tiled=True)
    mine = jnp.broadcast_to(jnp.sum(pieces, axis=0), part.shape)
    return lax.all_to_all(mine, "row", 0, 0, tiled=True)


def body(matrix, sources):
    rows, columns = matrix.shape
    slots = columns // BLOCK
    pairs = slots // 2
    row_count = lax.axis_size("row")
    total_rows = rows * row_count
    device = lax.axis_index("pair").astype(jnp.int32).reshape(1)
    f32 = partial(jax.ShapeDtypeStruct, dtype=F32)
    bf16 = partial(jax.ShapeDtypeStruct, dtype=BF16)
    square = (PAIR, PAIR)
    f, h = pltpu.VMEM(square, F32), pltpu.VMEM(square, BF16)
    work = [f, h, h, f, h, h, f, h, h, h, h, h, h, h, h] * pairs
    product_flops = 2 * PAIR**3 * 3
    part, high, low = call(
        first_gram,
        (f32((row_count, 2 * slots * BLOCK // 2 // row_count + 8, BLOCK)), bf16(matrix.shape), bf16(matrix.shape)),
        [VMEM],
        flops=3 * pairs * product_flops // 4,
    )(matrix)
    carried = ()
    for index in range(ROUNDS):
        last = index == ROUNDS - 1
        summed = sum_rows(part)
        block = f32((rows, BLOCK))
        out_shape = (f32((slots, rows, BLOCK)), block, block) + (bf16((pairs,) + square),) * 4
        kernel = first_rotate if index == 0 else partial(later_rotate, index, last)
        own, right, left, rh, rl, gh, gl = call(
            partial(kernel, total_rows, slots),
            out_shape,
            [SMEM, SMEM] + [VMEM] * (3 + len(carried)),
            work,
            flops=7 * pairs * product_flops,
        )(sources, device, summed, *carried, high, low)
        lower, upper = to_next(right, 1), to_next(left, -1)
        if last:
            return call(
                partial(settle, index, slots), f32(matrix.shape), [SMEM, SMEM] + [VMEM] * 3
            )(sources, device, own, lower, upper)
        small = f32((BLOCK, BLOCK))
        selves, self_right, self_left = call(
            partial(carry_self, index, slots),
            (f32((slots, BLOCK, BLOCK)), small, small),
            [SMEM, SMEM] + [VMEM] * 4,
            [pltpu.VMEM((PAIR, BLOCK), BF16)] * 2,
            flops=3 * pairs * product_flops // 2,
        )(sources, device, gh, gl, rh, rl)
        carried = (selves, to_next(self_right, 1), to_next(self_left, -1))
        part, high, low = call(
            partial(cross_gram, index, slots),
            (f32((row_count, pairs * BLOCK // row_count, BLOCK)), bf16(matrix.shape), bf16(matrix.shape)),
            [SMEM, SMEM] + [VMEM] * 3,
            flops=pairs * product_flops // 4,
        )(sources, device, own, lower, upper)


def solution(mesh):
    placed = (P("row", "pair"), P())
    return jax.shard_map(
        body, mesh=mesh, in_specs=placed, out_specs=P("row", "pair"), check_vma=False
    )
```

```python
from functools import partial

import jax
import jax.numpy as jnp
from jax import lax
from jax.experimental import pallas as pl
from jax.experimental.pallas import tpu as pltpu
from jax.sharding import PartitionSpec as P

BLOCK = 256
PAIR = 2 * BLOCK
ROUNDS = 3
F32 = jnp.float32
BF16 = jnp.bfloat16
POLY = (2.25, -2.4375, 1.6875, -0.5625, 0.0625)

VMEM = pl.BlockSpec(memory_space=pltpu.VMEM)
SMEM = pl.BlockSpec(memory_space=pltpu.SMEM)
ANY = pl.BlockSpec(memory_space=pl.ANY)


def call(kernel, out_shape, in_specs, scratch=(), flops=0, mib=10, out_spec=VMEM):
    return pl.pallas_call(
        kernel,
        out_shape=out_shape,
        in_specs=in_specs,
        out_specs=jax.tree.map(lambda _: out_spec, out_shape),
        scratch_shapes=list(scratch),
        compiler_params=pltpu.CompilerParams(vmem_limit_bytes=mib * 1024 * 1024),
        cost_estimate=pl.CostEstimate(flops=flops, bytes_accessed=4_000_000, transcendentals=0),
    )


def split(x):
    high = x.astype(BF16)
    return high, (x - high.astype(F32)).astype(BF16)


def dot(a, b):
    return jnp.dot(a, b, preferred_element_type=F32)


def dot_t(a, b):
    return lax.dot_general(a, b, (((0,), (0,)), ((), ())), preferred_element_type=F32)


def product(ah, al, bh, bl, cols, mul=dot):
    return mul(ah[...], bh[:, cols]) + (mul(ah[...], bl[:, cols]) + mul(al[...], bh[:, cols]))


def eye_mask(n):
    return lax.broadcasted_iota(jnp.int32, (n, n), 0) == lax.broadcasted_iota(jnp.int32, (n, n), 1)


def upper_mask(n):
    return lax.broadcasted_iota(jnp.int32, (n, n), 0) < lax.broadcasted_iota(jnp.int32, (n, n), 1)


def own_source(src_ref, dev_ref, round_index, slot, slots):
    base = dev_ref[0] * slots
    return src_ref[round_index, base + slot] - base


def leaving(src_ref, dev_ref, round_index, step, slots):
    base = dev_ref[0] * slots
    last = src_ref.shape[1] - slots
    there = jnp.clip(base + step * slots, 0, last)
    found = jnp.int32(0)
    for slot in range(slots):
        offset = src_ref[round_index, there + slot] - base
        found = jnp.where((offset >= 0) & (offset < slots), offset, found)
    return found


def picked(offset, slots, own_ref, lower_ref, upper_ref):
    own = own_ref[jnp.clip(offset, 0, slots - 1)]
    return jnp.where(offset < 0, lower_ref[...], jnp.where(offset >= slots, upper_ref[...], own))


def first_gram(a_ref, part_ref, high_ref, low_ref):
    pairs = a_ref.shape[1] // PAIR
    chunks = part_ref.shape[0]
    rows = part_ref.shape[1] - 8
    per = BLOCK // rows
    part_ref[:, rows:, :] = jnp.zeros((chunks, 8, BLOCK), F32)
    high, low = split(a_ref[...])
    high_ref[...] = high
    low_ref[...] = low
    for p in range(pairs):
        one, two = pl.ds(p * PAIR, BLOCK), pl.ds(p * PAIR + BLOCK, BLOCK)

        def gram(x, y):
            return dot_t(high_ref[:, x], high_ref[:, y]) + (
                dot_t(high_ref[:, x], low_ref[:, y]) + dot_t(low_ref[:, x], high_ref[:, y])
            )

        cross = gram(one, two)
        first = gram(one, one)
        second = gram(two, two)
        eye = eye_mask(BLOCK)
        diagonal = jnp.sum(jnp.where(eye, second, 0.0), axis=0, keepdims=True)
        both = jnp.where(eye | upper_mask(BLOCK), first, second)
        start = 2 * per * p
        for j in range(per):
            part_ref[start + j, :rows, :] = cross[j * rows:(j + 1) * rows]
            part_ref[start + per + j, :rows, :] = both[j * rows:(j + 1) * rows]
        part_ref[start, rows:, :] = jnp.broadcast_to(diagonal, (8, BLOCK))


def cross_gram(round_index, slots, src_ref, dev_ref, own_ref, lower_ref, upper_ref, after_ref, part_ref, high_ref, low_ref):
    rows = part_ref.shape[1]
    per = BLOCK // rows
    for slot in range(slots):
        offset = own_source(src_ref, dev_ref, round_index, slot, slots)
        high, low = split(picked(offset, slots, own_ref, lower_ref, upper_ref))
        high_ref[:, pl.ds(slot * BLOCK, BLOCK)] = high
        low_ref[:, pl.ds(slot * BLOCK, BLOCK)] = low
    for p in range(slots // 2):
        one, two = pl.ds(p * PAIR, BLOCK), pl.ds(p * PAIR + BLOCK, BLOCK)
        cross = dot_t(high_ref[:, one], high_ref[:, two]) + (
            dot_t(high_ref[:, one], low_ref[:, two]) + dot_t(low_ref[:, one], high_ref[:, two])
        )
        for j in range(per):
            part_ref[p * per + j] = cross[j * rows:(j + 1) * rows]


def set_generator(total_rows, cross, first, second, kf, kh, kl):
    eye = eye_mask(BLOCK)
    sign = jnp.where(eye, 0.0, jnp.where(upper_mask(BLOCK), 1.0, -1.0))
    scale = 1.0 / total_rows
    roots = []
    for block in (first, second):
        kept = jnp.where(eye, block * scale, 0.0)
        roots.append(
            (
                lax.rsqrt(jnp.sum(kept, axis=1, keepdims=True) + 1e-06),
                lax.rsqrt(jnp.sum(kept, axis=0, keepdims=True) + 1e-06),
            )
        )
    k11 = first * scale * roots[0][0] * roots[0][1] * sign
    k22 = second * scale * roots[1][0] * roots[1][1] * sign
    k12 = cross * scale * roots[0][0] * roots[1][1]
    total = jnp.sum(k11 * k11 + k22 * k22 + 2.0 * (k12 * k12), keepdims=True)
    lo, hi = pl.ds(0, BLOCK), pl.ds(BLOCK, BLOCK)
    for r, c, block in ((lo, lo, k11), (lo, hi, k12), (hi, lo, -k12.T), (hi, hi, k22)):
        kf[r, c] = block
        high, low = split(block)
        kh[r, c] = high
        kl[r, c] = low
    return 1.0 / (1.0 + jnp.sqrt(total))


def rotations(scales, work, out_high, out_low):
    pairs = len(scales)
    part = [pl.ds(0, BLOCK), pl.ds(BLOCK, BLOCK)]
    upper = [(p, i, j) for p in range(pairs) for i, j in ((0, 0), (0, 1), (1, 1))]
    coefficients = []
    for c in scales:
        u = c * c
        b0, b1, b2, b3, b4 = POLY
        coefficients.append(
            (
                u,
                b0 + u * (b1 + u * (b2 + u * (b3 + u * b4))),
                b1 + u * (2 * b2 + u * (3 * b3 + u * 4 * b4)),
                b2 + u * (3 * b3 + u * 6 * b4),
                b3 + u * 4 * b4,
                b4,
            )
        )

    def block(ah, al, bh, bl, i, j):
        r, c = part[i], part[j]
        return dot(ah[r, :], bh[:, c]) + (dot(ah[r, :], bl[:, c]) + dot(al[r, :], bh[:, c]))

    def put(high, low, i, j, value):
        high[part[i], part[j]], low[part[i], part[j]] = split(value)

    def put_symmetric(high, low, i, j, value):
        put(high, low, i, j, value)
        if i != j:
            put(high, low, j, i, value.T)

    for p, i, j in upper:
        kf, kh, kl, sf, sh, sl, vf, vh, vl, th, tl, xh, xl, yh, yl = work[p]
        s = -coefficients[p][0] * block(kh, kl, kh, kl, i, j)
        sf[part[i], part[j]] = s
        put_symmetric(sh, sl, i, j, s)
    for p, i, j in upper:
        kf, kh, kl, sf, sh, sl, vf, vh, vl, th, tl, xh, xl, yh, yl = work[p]
        u, a0, a1, a2, a3, a4 = coefficients[p]
        v = block(sh, sl, sh, sl, i, j)
        vf[part[i], part[j]] = v
        put_symmetric(vh, vl, i, j, v)
        put_symmetric(th, tl, i, j, a3 * sf[part[i], part[j]] + a4 * v)
    for p, i, j in upper:
        kf, kh, kl, sf, sh, sl, vf, vh, vl, th, tl, xh, xl, yh, yl = work[p]
        u, a0, a1, a2, a3, a4 = coefficients[p]
        t = a1 * sf[part[i], part[j]] + a2 * vf[part[i], part[j]] + block(vh, vl, th, tl, i, j)
        vf[part[i], part[j]] = t
        put_symmetric(sh, sl, i, j, t)
    for p, i, j in upper:
        kf, kh, kl, sf, sh, sl, vf, vh, vl, th, tl, xh, xl, yh, yl = work[p]
        u, a0, a1, a2, a3, a4 = coefficients[p]
        c = scales[p]
        odd = a0 * kf[part[i], part[j]] + block(kh, kl, sh, sl, i, j)
        even = vf[part[i], part[j]]
        if i == j:
            even = jnp.where(eye_mask(BLOCK), even + a0, even)
        x, y = c * (even - odd), c * (even + odd)
        sf[part[i], part[j]] = x
        put(xh, xl, i, j, x)
        put(yh, yl, i, j, y)
        if i != j:
            turned = y.T
            sf[part[j], part[i]] = turned
            put(xh, xl, j, i, turned)
            put(yh, yl, j, i, x.T)
    for p, i, j in upper:
        kf, kh, kl, sf, sh, sl, vf, vh, vl, th, tl, xh, xl, yh, yl = work[p]
        put_symmetric(vh, vl, i, j, block(yh, yl, xh, xl, i, j))
    for p in range(pairs):
        kf, kh, kl, sf, sh, sl, vf, vh, vl, th, tl, xh, xl, yh, yl = work[p]
        for cols in part:
            r = 1.5 * sf[:, cols] - 0.5 * product(xh, xl, vh, vl, cols)
            out_high[p, :, cols], out_low[p, :, cols] = split(r)


def apply(round_index, slots, src_ref, dev_ref, high_ref, low_ref, rh_ref, rl_ref, own_ref, right_ref, left_ref):
    for p in range(slots // 2):
        ah, al = high_ref.at[:, pl.ds(p * PAIR, PAIR)], low_ref.at[:, pl.ds(p * PAIR, PAIR)]
        for half in range(2):
            own_ref[2 * p + half] = product(ah, al, rh_ref.at[p], rl_ref.at[p], pl.ds(half * BLOCK, BLOCK))
    right_ref[...] = own_ref[leaving(src_ref, dev_ref, round_index, 1, slots)]
    left_ref[...] = own_ref[leaving(src_ref, dev_ref, round_index, -1, slots)]


def first_rotate(total_rows, slots, src_ref, dev_ref, sum_ref, high_ref, low_ref,
                 own_ref, right_ref, left_ref, rh_ref, rl_ref, gh_ref, gl_ref, *work):
    rows = sum_ref.shape[1] - 8
    per = BLOCK // rows
    work = [work[15 * p:15 * p + 15] for p in range(slots // 2)]
    scales = []
    lo, hi = pl.ds(0, BLOCK), pl.ds(BLOCK, BLOCK)
    for p in range(slots // 2):
        start = 2 * per * p
        cross = sum_ref[start:start + per, :rows, :].reshape(BLOCK, BLOCK)
        both = sum_ref[start + per:start + 2 * per, :rows, :].reshape(BLOCK, BLOCK)
        diagonal = sum_ref[start, rows:rows + 1, :]
        turned = both.T
        eye, upper = eye_mask(BLOCK), upper_mask(BLOCK)
        first = jnp.where(eye | upper, both, turned)
        second = jnp.where(eye, diagonal, jnp.where(upper, turned, both))
        for r, c, block in ((lo, lo, first), (lo, hi, cross), (hi, lo, cross.T), (hi, hi, second)):
            high, low = split(block)
            gh_ref[p, r, c] = high
            gl_ref[p, r, c] = low
        scales.append(set_generator(total_rows, cross, first, second, *work[p][:3]))
    rotations(scales, work, rh_ref, rl_ref)
    apply(0, slots, src_ref, dev_ref, high_ref, low_ref, rh_ref, rl_ref, own_ref, right_ref, left_ref)


def later_rotate(round_index, last, total_rows, slots, src_ref, dev_ref, sum_ref, self_ref, lower_ref, upper_ref,
                 high_ref, low_ref, own_ref, right_ref, left_ref, rh_ref, rl_ref, gh_ref, gl_ref, *work):
    rows = sum_ref.shape[1]
    per = BLOCK // rows
    work = [work[15 * p:15 * p + 15] for p in range(slots // 2)]
    scales = []
    lo, hi = pl.ds(0, BLOCK), pl.ds(BLOCK, BLOCK)
    for p in range(slots // 2):
        cross = sum_ref[p * per:p * per + per].reshape(BLOCK, BLOCK)
        first, second = (
            picked(own_source(src_ref, dev_ref, round_index - 1, 2 * p + half, slots), slots, self_ref, lower_ref, upper_ref)
            for half in range(2)
        )
        if not last:
            for r, c, block in ((lo, lo, first), (lo, hi, cross), (hi, lo, cross.T), (hi, hi, second)):
                high, low = split(block)
                gh_ref[p, r, c] = high
                gl_ref[p, r, c] = low
        scales.append(set_generator(total_rows, cross, first, second, *work[p][:3]))
    rotations(scales, work, rh_ref, rl_ref)
    apply(round_index, slots, src_ref, dev_ref, high_ref, low_ref, rh_ref, rl_ref, own_ref, right_ref, left_ref)


def carry_self(round_index, slots, src_ref, dev_ref, gh_ref, gl_ref, rh_ref, rl_ref,
               self_ref, right_ref, left_ref, yh, yl):
    for p in range(slots // 2):
        for half in range(2):
            cols = pl.ds(half * BLOCK, BLOCK)
            yh[...], yl[...] = split(product(gh_ref.at[p], gl_ref.at[p], rh_ref.at[p], rl_ref.at[p], cols))
            self_ref[2 * p + half] = dot_t(rh_ref[p, :, cols], yh[...]) + (
                dot_t(rh_ref[p, :, cols], yl[...]) + dot_t(rl_ref[p, :, cols], yh[...])
            )
    right_ref[...] = self_ref[leaving(src_ref, dev_ref, round_index, 1, slots)]
    left_ref[...] = self_ref[leaving(src_ref, dev_ref, round_index, -1, slots)]


def settle(round_index, slots, src_ref, dev_ref, own_ref, lower_ref, upper_ref, out_ref, sems):
    for slot in range(slots):
        offset = own_source(src_ref, dev_ref, round_index, slot, slots)
        goal = out_ref.at[:, pl.ds(slot * BLOCK, BLOCK)]

        @pl.when(offset < 0)
        def _():
            pltpu.make_async_copy(lower_ref, goal, sems.at[slot]).start()

        @pl.when(offset >= slots)
        def _():
            pltpu.make_async_copy(upper_ref, goal, sems.at[slot]).start()

        @pl.when((offset >= 0) & (offset < slots))
        def _():
            kept = own_ref.at[jnp.clip(offset, 0, slots - 1)]
            pltpu.make_async_copy(kept, goal, sems.at[slot]).start()

    for slot in range(slots):
        goal = out_ref.at[:, pl.ds(slot * BLOCK, BLOCK)]
        pltpu.make_async_copy(lower_ref, goal, sems.at[slot]).wait()


def to_next(x, by):
    count = lax.axis_size("pair")
    return lax.ppermute(x, "pair", [(i, (i + by) % count) for i in range(count)])


def sum_rows(part):
    pieces = lax.all_to_all(part, "row", 0, 0, tiled=True)
    mine = jnp.broadcast_to(jnp.sum(pieces, axis=0), part.shape)
    return lax.all_to_all(mine, "row", 0, 0, tiled=True)


def body(matrix, sources):
    rows, columns = matrix.shape
    slots = columns // BLOCK
    pairs = slots // 2
    row_count = lax.axis_size("row")
    total_rows = rows * row_count
    device = lax.axis_index("pair").astype(jnp.int32).reshape(1)
    f32 = partial(jax.ShapeDtypeStruct, dtype=F32)
    bf16 = partial(jax.ShapeDtypeStruct, dtype=BF16)
    square = (PAIR, PAIR)
    f, h = pltpu.VMEM(square, F32), pltpu.VMEM(square, BF16)
    work = [f, h, h, f, h, h, f, h, h, h, h, h, h, h, h] * pairs
    product_flops = 2 * PAIR**3 * 3
    part, high, low = call(
        first_gram,
        (f32((row_count, 2 * slots * BLOCK // 2 // row_count + 8, BLOCK)), bf16(matrix.shape), bf16(matrix.shape)),
        [VMEM],
        flops=3 * pairs * product_flops // 4,
    )(matrix)
    carried = ()
    for index in range(ROUNDS):
        last = index == ROUNDS - 1
        summed = sum_rows(part)
        block = f32((rows, BLOCK))
        out_shape = (f32((slots, rows, BLOCK)), block, block) + (bf16((pairs,) + square),) * 4
        kernel = first_rotate if index == 0 else partial(later_rotate, index, last)
        own, right, left, rh, rl, gh, gl = call(
            partial(kernel, total_rows, slots),
            out_shape,
            [SMEM, SMEM] + [VMEM] * (3 + len(carried)),
            work,
            flops=7 * pairs * product_flops,
            mib=26,
        )(sources, device, summed, *carried, high, low)
        lower, upper = to_next(right, 1), to_next(left, -1)
        if last:
            return call(
                partial(settle, index, slots),
                f32(matrix.shape),
                [SMEM, SMEM] + [VMEM] * 3,
                [pltpu.SemaphoreType.DMA((slots,))],
                out_spec=ANY,
            )(sources, device, own, lower, upper)
        small = f32((BLOCK, BLOCK))
        selves, self_right, self_left = call(
            partial(carry_self, index, slots),
            (f32((slots, BLOCK, BLOCK)), small, small),
            [SMEM, SMEM] + [VMEM] * 4,
            [pltpu.VMEM((PAIR, BLOCK), BF16)] * 2,
            flops=3 * pairs * product_flops // 2,
        )(sources, device, gh, gl, rh, rl)
        carried = (selves, to_next(self_right, 1), to_next(self_left, -1))
        part, high, low = call(
            partial(cross_gram, index, slots),
            (f32((row_count, pairs * BLOCK // row_count, BLOCK)), bf16(matrix.shape), bf16(matrix.shape)),
            [SMEM, SMEM] + [VMEM] * 3 + [ANY],
            flops=pairs * product_flops // 4,
        )(sources, device, own, lower, upper, selves)


def solution(mesh):
    placed = (P("row", "pair"), P())
    return jax.shard_map(
        body, mesh=mesh, in_specs=placed, out_specs=P("row", "pair"), check_vma=False
    )
```

```python
from functools import partial

import jax
import jax.numpy as jnp
from jax import lax
from jax.experimental import pallas as pl
from jax.experimental.pallas import tpu as pltpu
from jax.sharding import PartitionSpec as P

BLOCK = 256
PAIR = 2 * BLOCK
ROUNDS = 3
F32 = jnp.float32
BF16 = jnp.bfloat16
POLY = (2.25, -2.4375, 1.6875, -0.5625, 0.0625)

VMEM = pl.BlockSpec(memory_space=pltpu.VMEM)
SMEM = pl.BlockSpec(memory_space=pltpu.SMEM)
ANY = pl.BlockSpec(memory_space=pl.ANY)


def call(kernel, out_shape, in_specs, scratch=(), flops=0, mib=10, out_spec=VMEM, alias=None):
    return pl.pallas_call(
        kernel,
        out_shape=out_shape,
        in_specs=in_specs,
        out_specs=jax.tree.map(lambda _: out_spec, out_shape),
        scratch_shapes=list(scratch),
        input_output_aliases=alias or {},
        compiler_params=pltpu.CompilerParams(vmem_limit_bytes=mib * 1024 * 1024),
        cost_estimate=pl.CostEstimate(flops=flops, bytes_accessed=4_000_000, transcendentals=0),
    )


def split(x):
    high = x.astype(BF16)
    return high, (x - high.astype(F32)).astype(BF16)


def dot(a, b):
    return jnp.dot(a, b, preferred_element_type=F32)


def dot_t(a, b):
    return lax.dot_general(a, b, (((0,), (0,)), ((), ())), preferred_element_type=F32)


def product(ah, al, bh, bl, cols, mul=dot):
    return mul(ah[...], bh[:, cols]) + (mul(ah[...], bl[:, cols]) + mul(al[...], bh[:, cols]))


def eye_mask(n):
    return lax.broadcasted_iota(jnp.int32, (n, n), 0) == lax.broadcasted_iota(jnp.int32, (n, n), 1)


def upper_mask(n):
    return lax.broadcasted_iota(jnp.int32, (n, n), 0) < lax.broadcasted_iota(jnp.int32, (n, n), 1)


def own_source(src_ref, dev_ref, round_index, slot, slots):
    base = dev_ref[0] * slots
    return src_ref[round_index, base + slot] - base


def leaving(src_ref, dev_ref, round_index, step, slots):
    base = dev_ref[0] * slots
    last = src_ref.shape[1] - slots
    there = jnp.clip(base + step * slots, 0, last)
    found = jnp.int32(0)
    for slot in range(slots):
        offset = src_ref[round_index, there + slot] - base
        found = jnp.where((offset >= 0) & (offset < slots), offset, found)
    return found


def picked(offset, slots, own_ref, lower_ref, upper_ref):
    own = own_ref[jnp.clip(offset, 0, slots - 1)]
    return jnp.where(offset < 0, lower_ref[...], jnp.where(offset >= slots, upper_ref[...], own))


def first_gram(a_ref, part_ref, high_ref, low_ref):
    pairs = a_ref.shape[1] // PAIR
    chunks = part_ref.shape[0]
    rows = part_ref.shape[1] - 8
    per = BLOCK // rows
    part_ref[:, rows:, :] = jnp.zeros((chunks, 8, BLOCK), F32)
    for p in range(pairs):
        one, two = pl.ds(p * PAIR, BLOCK), pl.ds(p * PAIR + BLOCK, BLOCK)
        for cols in (one, two):
            high_ref[:, cols], low_ref[:, cols] = split(a_ref[:, cols])

        def gram(x, y):
            return dot_t(high_ref[:, x], high_ref[:, y]) + (
                dot_t(high_ref[:, x], low_ref[:, y]) + dot_t(low_ref[:, x], high_ref[:, y])
            )

        cross = gram(one, two)
        first = gram(one, one)
        second = gram(two, two)
        eye = eye_mask(BLOCK)
        diagonal = jnp.sum(jnp.where(eye, second, 0.0), axis=0, keepdims=True)
        both = jnp.where(eye | upper_mask(BLOCK), first, second)
        start = 2 * per * p
        for j in range(per):
            part_ref[start + j, :rows, :] = cross[j * rows:(j + 1) * rows]
            part_ref[start + per + j, :rows, :] = both[j * rows:(j + 1) * rows]
        part_ref[start, rows:, :] = jnp.broadcast_to(diagonal, (8, BLOCK))


def cross_gram(round_index, slots, src_ref, dev_ref, own_ref, lower_ref, upper_ref, part_ref, high_ref, low_ref):
    rows = part_ref.shape[1]
    per = BLOCK // rows
    for slot in range(slots):
        offset = own_source(src_ref, dev_ref, round_index, slot, slots)
        high, low = split(picked(offset, slots, own_ref, lower_ref, upper_ref))
        high_ref[:, pl.ds(slot * BLOCK, BLOCK)] = high
        low_ref[:, pl.ds(slot * BLOCK, BLOCK)] = low
    for p in range(slots // 2):
        one, two = pl.ds(p * PAIR, BLOCK), pl.ds(p * PAIR + BLOCK, BLOCK)
        cross = dot_t(high_ref[:, one], high_ref[:, two]) + (
            dot_t(high_ref[:, one], low_ref[:, two]) + dot_t(low_ref[:, one], high_ref[:, two])
        )
        for j in range(per):
            part_ref[p * per + j] = cross[j * rows:(j + 1) * rows]


def set_generator(total_rows, cross, first, second, kf, kh, kl):
    eye = eye_mask(BLOCK)
    sign = jnp.where(eye, 0.0, jnp.where(upper_mask(BLOCK), 1.0, -1.0))
    scale = 1.0 / total_rows
    roots = []
    for block in (first, second):
        kept = jnp.where(eye, block * scale, 0.0)
        roots.append(
            (
                lax.rsqrt(jnp.sum(kept, axis=1, keepdims=True) + 1e-06),
                lax.rsqrt(jnp.sum(kept, axis=0, keepdims=True) + 1e-06),
            )
        )
    k11 = first * scale * roots[0][0] * roots[0][1] * sign
    k22 = second * scale * roots[1][0] * roots[1][1] * sign
    k12 = cross * scale * roots[0][0] * roots[1][1]
    total = jnp.sum(k11 * k11 + k22 * k22 + 2.0 * (k12 * k12), keepdims=True)
    lo, hi = pl.ds(0, BLOCK), pl.ds(BLOCK, BLOCK)
    for r, c, block in ((lo, lo, k11), (lo, hi, k12), (hi, lo, -k12.T), (hi, hi, k22)):
        kf[r, c] = block
        high, low = split(block)
        kh[r, c] = high
        kl[r, c] = low
    return 1.0 / (1.0 + jnp.sqrt(total))


def rotations(generator, work, out_high, out_low):
    pairs = len(work)
    part = [pl.ds(0, BLOCK), pl.ds(BLOCK, BLOCK)]
    upper = ((0, 0), (0, 1), (1, 1))
    scales, coefficients = {}, {}

    def start(p):
        c = generator(p)
        u = c * c
        b0, b1, b2, b3, b4 = POLY
        scales[p] = c
        coefficients[p] = (
            u,
            b0 + u * (b1 + u * (b2 + u * (b3 + u * b4))),
            b1 + u * (2 * b2 + u * (3 * b3 + u * 4 * b4)),
            b2 + u * (3 * b3 + u * 6 * b4),
            b3 + u * 4 * b4,
            b4,
        )

    def block(ah, al, bh, bl, i, j):
        r, c = part[i], part[j]
        return dot(ah[r, :], bh[:, c]) + (dot(ah[r, :], bl[:, c]) + dot(al[r, :], bh[:, c]))

    def put(high, low, i, j, value):
        high[part[i], part[j]], low[part[i], part[j]] = split(value)

    def put_symmetric(high, low, i, j, value):
        put(high, low, i, j, value)
        if i != j:
            put(high, low, j, i, value.T)

    def square(p):
        kf, kh, kl, sf, sh, sl, vf, vh, vl, th, tl, xh, xl, yh, yl = work[p]
        for i, j in upper:
            s = -coefficients[p][0] * block(kh, kl, kh, kl, i, j)
            sf[part[i], part[j]] = s
            put_symmetric(sh, sl, i, j, s)

    def fourth(p):
        kf, kh, kl, sf, sh, sl, vf, vh, vl, th, tl, xh, xl, yh, yl = work[p]
        u, a0, a1, a2, a3, a4 = coefficients[p]
        for i, j in upper:
            v = block(sh, sl, sh, sl, i, j)
            vf[part[i], part[j]] = v
            put_symmetric(vh, vl, i, j, v)
            put_symmetric(th, tl, i, j, a3 * sf[part[i], part[j]] + a4 * v)

    def polynomial(p):
        kf, kh, kl, sf, sh, sl, vf, vh, vl, th, tl, xh, xl, yh, yl = work[p]
        u, a0, a1, a2, a3, a4 = coefficients[p]
        for i, j in upper:
            t = a1 * sf[part[i], part[j]] + a2 * vf[part[i], part[j]] + block(vh, vl, th, tl, i, j)
            vf[part[i], part[j]] = t
            put_symmetric(sh, sl, i, j, t)

    def second(p):
        kf, kh, kl, sf, sh, sl, vf, vh, vl, th, tl, xh, xl, yh, yl = work[p]
        u, a0, a1, a2, a3, a4 = coefficients[p]
        c = scales[p]
        for i, j in upper:
            odd = a0 * kf[part[i], part[j]] + block(kh, kl, sh, sl, i, j)
            even = vf[part[i], part[j]]
            if i == j:
                even = jnp.where(eye_mask(BLOCK), even + a0, even)
            x, y = c * (even - odd), c * (even + odd)
            sf[part[i], part[j]] = x
            put(xh, xl, i, j, x)
            put(yh, yl, i, j, y)
            if i != j:
                turned = y.T
                sf[part[j], part[i]] = turned
                put(xh, xl, j, i, turned)
                put(yh, yl, j, i, x.T)

    def metric(p):
        kf, kh, kl, sf, sh, sl, vf, vh, vl, th, tl, xh, xl, yh, yl = work[p]
        for i, j in upper:
            put_symmetric(vh, vl, i, j, block(yh, yl, xh, xl, i, j))

    def third(p):
        kf, kh, kl, sf, sh, sl, vf, vh, vl, th, tl, xh, xl, yh, yl = work[p]
        for cols in part:
            r = 1.5 * sf[:, cols] - 0.5 * product(xh, xl, vh, vl, cols)
            out_high[p, :, cols], out_low[p, :, cols] = split(r)

    stages = (start, square, fourth, polynomial, second, metric, third)
    for step in range(len(stages) + pairs - 1):
        for p in range(pairs):
            if 0 <= step - p < len(stages):
                stages[step - p](p)


def leave(round_index, slots, src_ref, dev_ref, high_ref, low_ref, rh_ref, rl_ref, right_ref, left_ref):
    for step, out_ref in ((1, right_ref), (-1, left_ref)):
        slot = leaving(src_ref, dev_ref, round_index, step, slots)
        pair, half = slot >> 1, slot & 1
        rows = pl.ds(pl.multiple_of(pair * PAIR, PAIR), PAIR)
        cols = pl.ds(pl.multiple_of(half * BLOCK, BLOCK), BLOCK)
        out_ref[...] = product(
            high_ref.at[:, rows], low_ref.at[:, rows], rh_ref.at[pair], rl_ref.at[pair], cols
        )


def first_rotate(total_rows, slots, src_ref, dev_ref, sum_ref, high_ref, low_ref,
                 right_ref, left_ref, rh_ref, rl_ref, gh_ref, gl_ref, *work):
    rows = sum_ref.shape[1] - 8
    per = BLOCK // rows
    work = [work[15 * p:15 * p + 15] for p in range(slots // 2)]
    lo, hi = pl.ds(0, BLOCK), pl.ds(BLOCK, BLOCK)

    def generator(p):
        start = 2 * per * p
        cross = sum_ref[start:start + per, :rows, :].reshape(BLOCK, BLOCK)
        both = sum_ref[start + per:start + 2 * per, :rows, :].reshape(BLOCK, BLOCK)
        diagonal = sum_ref[start, rows:rows + 1, :]
        turned = both.T
        eye, upper = eye_mask(BLOCK), upper_mask(BLOCK)
        first = jnp.where(eye | upper, both, turned)
        second = jnp.where(eye, diagonal, jnp.where(upper, turned, both))
        for r, c, block in ((lo, lo, first), (lo, hi, cross), (hi, lo, cross.T), (hi, hi, second)):
            high, low = split(block)
            gh_ref[p, r, c] = high
            gl_ref[p, r, c] = low
        return set_generator(total_rows, cross, first, second, *work[p][:3])

    rotations(generator, work, rh_ref, rl_ref)
    leave(0, slots, src_ref, dev_ref, high_ref, low_ref, rh_ref, rl_ref, right_ref, left_ref)


def later_rotate(round_index, last, total_rows, slots, src_ref, dev_ref, sum_ref, self_ref,
                 high_ref, low_ref, right_ref, left_ref, rh_ref, rl_ref, *rest):
    rows = sum_ref.shape[1]
    per = BLOCK // rows
    if not last:
        gh_ref, gl_ref = rest[:2]
    work = rest[-15 * (slots // 2):]
    work = [work[15 * p:15 * p + 15] for p in range(slots // 2)]
    lo, hi = pl.ds(0, BLOCK), pl.ds(BLOCK, BLOCK)

    def generator(p):
        cross = sum_ref[p * per:p * per + per].reshape(BLOCK, BLOCK)
        first, second = self_ref[2 * p], self_ref[2 * p + 1]
        if not last:
            for r, c, block in ((lo, lo, first), (lo, hi, cross), (hi, lo, cross.T), (hi, hi, second)):
                high, low = split(block)
                gh_ref[p, r, c] = high
                gl_ref[p, r, c] = low
        return set_generator(total_rows, cross, first, second, *work[p][:3])

    rotations(generator, work, rh_ref, rl_ref)
    leave(round_index, slots, src_ref, dev_ref, high_ref, low_ref, rh_ref, rl_ref, right_ref, left_ref)


def carry_self(round_index, slots, src_ref, dev_ref, gh_ref, gl_ref, rh_ref, rl_ref,
               self_ref, right_ref, left_ref, *work):
    for slot in range(slots):
        p, cols = slot // 2, pl.ds(slot % 2 * BLOCK, BLOCK)
        yh, yl = work[2 * slot:2 * slot + 2]
        yh[...], yl[...] = split(product(gh_ref.at[p], gl_ref.at[p], rh_ref.at[p], rl_ref.at[p], cols))
    for slot in range(slots):
        p, cols = slot // 2, pl.ds(slot % 2 * BLOCK, BLOCK)
        yh, yl = work[2 * slot:2 * slot + 2]
        self_ref[slot] = dot_t(rh_ref[p, :, cols], yh[...]) + (
            dot_t(rh_ref[p, :, cols], yl[...]) + dot_t(rl_ref[p, :, cols], yh[...])
        )
    right_ref[...] = self_ref[leaving(src_ref, dev_ref, round_index, 1, slots)]
    left_ref[...] = self_ref[leaving(src_ref, dev_ref, round_index, -1, slots)]


def take_self(round_index, slots, src_ref, dev_ref, self_ref, lower_ref, upper_ref, after_ref, out_ref):
    for slot in range(slots):
        offset = own_source(src_ref, dev_ref, round_index, slot, slots)
        out_ref[slot] = picked(offset, slots, self_ref, lower_ref, upper_ref)


def apply(slots, high_ref, low_ref, rh_ref, rl_ref, after_ref, own_ref):
    for slot in range(slots):
        p, cols = slot // 2, pl.ds(slot % 2 * BLOCK, BLOCK)
        rows = pl.ds(p * PAIR, PAIR)
        own_ref[slot] = product(high_ref.at[:, rows], low_ref.at[:, rows], rh_ref.at[p], rl_ref.at[p], cols)


def apply_last(round_index, slots, src_ref, dev_ref, high_ref, low_ref, rh_ref, rl_ref, out_ref, own_ref, sems):
    apply(slots, high_ref, low_ref, rh_ref, rl_ref, None, own_ref)
    offsets = [own_source(src_ref, dev_ref, round_index, slot, slots) for slot in range(slots)]
    for wait in (False, True):
        for slot, offset in enumerate(offsets):
            @pl.when((offset >= 0) & (offset < slots))
            def _():
                kept = own_ref.at[jnp.clip(offset, 0, slots - 1)]
                goal = out_ref.at[:, pl.ds(slot * BLOCK, BLOCK)]
                copy = pltpu.make_async_copy(kept, goal, sems.at[slot])
                copy.wait() if wait else copy.start()


def settle(round_index, slots, src_ref, dev_ref, most_ref, lower_ref, upper_ref, out_ref, sems):
    offsets = [own_source(src_ref, dev_ref, round_index, slot, slots) for slot in range(slots)]
    for wait in (False, True):
        for slot, offset in enumerate(offsets):
            goal = out_ref.at[:, pl.ds(slot * BLOCK, BLOCK)]

            @pl.when(offset < 0)
            def _():
                copy = pltpu.make_async_copy(lower_ref, goal, sems.at[slot])
                copy.wait() if wait else copy.start()

            @pl.when(offset >= slots)
            def _():
                copy = pltpu.make_async_copy(upper_ref, goal, sems.at[slot])
                copy.wait() if wait else copy.start()


def to_next(x, by):
    count = lax.axis_size("pair")
    return lax.ppermute(x, "pair", [(i, (i + by) % count) for i in range(count)])


def add_up(pieces_ref, out_ref):
    total = jnp.sum(pieces_ref[...], axis=0)
    for chunk in range(out_ref.shape[0]):
        out_ref[chunk] = total


def sum_rows(part):
    pieces = lax.all_to_all(part, "row", 0, 0, tiled=True)
    mine = call(add_up, jax.ShapeDtypeStruct(part.shape, F32), [VMEM])(pieces)
    return lax.all_to_all(mine, "row", 0, 0, tiled=True)


def body(matrix, sources):
    rows, columns = matrix.shape
    slots = columns // BLOCK
    pairs = slots // 2
    row_count = lax.axis_size("row")
    total_rows = rows * row_count
    device = lax.axis_index("pair").astype(jnp.int32).reshape(1)
    f32 = partial(jax.ShapeDtypeStruct, dtype=F32)
    bf16 = partial(jax.ShapeDtypeStruct, dtype=BF16)
    square = (PAIR, PAIR)
    f, h = pltpu.VMEM(square, F32), pltpu.VMEM(square, BF16)
    work = [f, h, h, f, h, h, f, h, h, h, h, h, h, h, h] * pairs
    product_flops = 2 * PAIR**3 * 3
    sems = pltpu.SemaphoreType.DMA((slots,))
    part, high, low = call(
        first_gram,
        (f32((row_count, 2 * slots * BLOCK // 2 // row_count + 8, BLOCK)), bf16(matrix.shape), bf16(matrix.shape)),
        [VMEM],
        flops=3 * pairs * product_flops // 4,
    )(matrix)
    part, sources, device = lax.optimization_barrier((part, sources, device))
    block, small = f32((rows, BLOCK)), f32((BLOCK, BLOCK))
    carried = ()
    for index in range(ROUNDS):
        last = index == ROUNDS - 1
        summed = sum_rows(part)
        kernel = first_rotate if index == 0 else partial(later_rotate, index, last)
        right, left, rh, rl, *gram = call(
            partial(kernel, total_rows, slots),
            (block, block) + (bf16((pairs,) + square),) * (2 if last else 4),
            [SMEM, SMEM] + [VMEM] * (3 + len(carried)),
            work,
            flops=7 * pairs * product_flops,
            mib=20,
        )(sources, device, summed, *carried, high, low)
        lower, upper = to_next(right, 1), to_next(left, -1)
        if last:
            most = call(
                partial(apply_last, index, slots),
                f32(matrix.shape),
                [SMEM, SMEM] + [VMEM] * 4,
                [pltpu.VMEM((slots, rows, BLOCK), F32), sems],
                flops=pairs * product_flops,
                out_spec=ANY,
            )(sources, device, high, low, rh, rl)
            return call(
                partial(settle, index, slots),
                f32(matrix.shape),
                [SMEM, SMEM, ANY, VMEM, VMEM],
                [sems],
                out_spec=ANY,
                alias={2: 0},
            )(sources, device, most, lower, upper)
        selves, self_right, self_left = call(
            partial(carry_self, index, slots),
            (f32((slots, BLOCK, BLOCK)), small, small),
            [SMEM, SMEM] + [VMEM] * 4,
            [pltpu.VMEM((PAIR, BLOCK), BF16)] * (2 * slots),
            flops=3 * pairs * product_flops // 2,
        )(sources, device, *gram, rh, rl)
        own = call(
            partial(apply, slots),
            f32((slots, rows, BLOCK)),
            [VMEM] * 4 + [ANY],
            flops=pairs * product_flops,
        )(high, low, rh, rl, selves)
        lower_self, upper_self = to_next(self_right, 1), to_next(self_left, -1)
        part, high, low = call(
            partial(cross_gram, index, slots),
            (f32((row_count, pairs * BLOCK // row_count, BLOCK)), bf16(matrix.shape), bf16(matrix.shape)),
            [SMEM, SMEM] + [VMEM] * 3,
            flops=pairs * product_flops // 4,
        )(sources, device, own, lower, upper)
        selves = call(
            partial(take_self, index, slots), f32((slots, BLOCK, BLOCK)), [SMEM, SMEM] + [VMEM] * 3 + [ANY]
        )(sources, device, selves, lower_self, upper_self, part)
        part, *carried = lax.optimization_barrier((part, selves))


def solution(mesh):
    placed = (P("row", "pair"), P())
    return jax.shard_map(
        body, mesh=mesh, in_specs=placed, out_specs=P("row", "pair"), check_vma=False
    )
```

```python
from functools import partial

import jax
import jax.numpy as jnp
from jax import lax
from jax.experimental import pallas as pl
from jax.experimental.pallas import tpu as pltpu
from jax.sharding import PartitionSpec as P

BLOCK = 256
PAIR = 2 * BLOCK
ROUNDS = 3
UNROLLED = (0, 1, 2)
F32 = jnp.float32
BF16 = jnp.bfloat16
POLY = (2.25, -2.4375, 1.6875, -0.5625, 0.0625)

VMEM = pl.BlockSpec(memory_space=pltpu.VMEM)
SMEM = pl.BlockSpec(memory_space=pltpu.SMEM)
ANY = pl.BlockSpec(memory_space=pl.ANY)


def call(kernel, out_shape, in_specs, scratch=(), flops=0, mib=10, out_spec=VMEM, alias=None):
    return pl.pallas_call(
        kernel,
        out_shape=out_shape,
        in_specs=in_specs,
        out_specs=jax.tree.map(lambda _: out_spec, out_shape),
        scratch_shapes=list(scratch),
        input_output_aliases=alias or {},
        compiler_params=pltpu.CompilerParams(vmem_limit_bytes=mib * 1024 * 1024),
        cost_estimate=pl.CostEstimate(flops=flops, bytes_accessed=4_000_000, transcendentals=0),
    )


def split(x):
    high = x.astype(BF16)
    return high, (x - high.astype(F32)).astype(BF16)


def dot(a, b):
    return jnp.dot(a, b, preferred_element_type=F32)


def dot_t(a, b):
    return lax.dot_general(a, b, (((0,), (0,)), ((), ())), preferred_element_type=F32)


def product(ah, al, bh, bl, cols, mul=dot):
    return mul(ah[...], bh[:, cols]) + (mul(ah[...], bl[:, cols]) + mul(al[...], bh[:, cols]))


def eye_mask(n):
    return lax.broadcasted_iota(jnp.int32, (n, n), 0) == lax.broadcasted_iota(jnp.int32, (n, n), 1)


def upper_mask(n):
    return lax.broadcasted_iota(jnp.int32, (n, n), 0) < lax.broadcasted_iota(jnp.int32, (n, n), 1)


def own_source(src_ref, dev_ref, round_index, slot, slots):
    base = dev_ref[0] * slots
    return src_ref[round_index, base + slot] - base


def leaving(src_ref, dev_ref, round_index, step, slots):
    base = dev_ref[0] * slots
    last = src_ref.shape[1] - slots
    there = jnp.clip(base + step * slots, 0, last)
    found = jnp.int32(0)
    for slot in range(slots):
        offset = src_ref[round_index, there + slot] - base
        found = jnp.where((offset >= 0) & (offset < slots), offset, found)
    return found


def picked(offset, slots, own_ref, lower_ref, upper_ref):
    own = own_ref[jnp.clip(offset, 0, slots - 1)]
    return jnp.where(offset < 0, lower_ref[...], jnp.where(offset >= slots, upper_ref[...], own))


def first_gram(a_ref, part_ref, high_ref, low_ref):
    pairs = a_ref.shape[1] // PAIR
    chunks = part_ref.shape[0]
    rows = part_ref.shape[1] - 8
    per = BLOCK // rows
    part_ref[:, rows:, :] = jnp.zeros((chunks, 8, BLOCK), F32)
    for p in range(pairs):
        one, two = pl.ds(p * PAIR, BLOCK), pl.ds(p * PAIR + BLOCK, BLOCK)
        for cols in (one, two):
            high_ref[:, cols], low_ref[:, cols] = split(a_ref[:, cols])

        def gram(x, y):
            return dot_t(high_ref[:, x], high_ref[:, y]) + (
                dot_t(high_ref[:, x], low_ref[:, y]) + dot_t(low_ref[:, x], high_ref[:, y])
            )

        cross = gram(one, two)
        first = gram(one, one)
        second = gram(two, two)
        eye = eye_mask(BLOCK)
        diagonal = jnp.sum(jnp.where(eye, second, 0.0), axis=0, keepdims=True)
        both = jnp.where(eye | upper_mask(BLOCK), first, second)
        start = 2 * per * p
        for j in range(per):
            part_ref[start + j, :rows, :] = cross[j * rows:(j + 1) * rows]
            part_ref[start + per + j, :rows, :] = both[j * rows:(j + 1) * rows]
        part_ref[start, rows:, :] = jnp.broadcast_to(diagonal, (8, BLOCK))


def cross_gram(round_index, slots, src_ref, dev_ref, own_ref, lower_ref, upper_ref, part_ref, high_ref, low_ref):
    rows = part_ref.shape[1]
    per = BLOCK // rows
    for slot in range(slots):
        offset = own_source(src_ref, dev_ref, round_index, slot, slots)
        high, low = split(picked(offset, slots, own_ref, lower_ref, upper_ref))
        high_ref[:, pl.ds(slot * BLOCK, BLOCK)] = high
        low_ref[:, pl.ds(slot * BLOCK, BLOCK)] = low
    for p in range(slots // 2):
        one, two = pl.ds(p * PAIR, BLOCK), pl.ds(p * PAIR + BLOCK, BLOCK)
        cross = dot_t(high_ref[:, one], high_ref[:, two]) + (
            dot_t(high_ref[:, one], low_ref[:, two]) + dot_t(low_ref[:, one], high_ref[:, two])
        )
        for j in range(per):
            part_ref[p * per + j] = cross[j * rows:(j + 1) * rows]


def set_generator(total_rows, cross, first, second, kf, kh, kl):
    eye = eye_mask(BLOCK)
    sign = jnp.where(eye, 0.0, jnp.where(upper_mask(BLOCK), 1.0, -1.0))
    scale = 1.0 / total_rows
    roots = []
    for block in (first, second):
        kept = jnp.where(eye, block * scale, 0.0)
        roots.append(
            (
                lax.rsqrt(jnp.sum(kept, axis=1, keepdims=True) + 1e-06),
                lax.rsqrt(jnp.sum(kept, axis=0, keepdims=True) + 1e-06),
            )
        )
    k11 = first * scale * roots[0][0] * roots[0][1] * sign
    k22 = second * scale * roots[1][0] * roots[1][1] * sign
    k12 = cross * scale * roots[0][0] * roots[1][1]
    total = jnp.sum(k11 * k11 + k22 * k22 + 2.0 * (k12 * k12), keepdims=True)
    lo, hi = pl.ds(0, BLOCK), pl.ds(BLOCK, BLOCK)
    for r, c, block in ((lo, lo, k11), (lo, hi, k12), (hi, lo, -k12.T), (hi, hi, k22)):
        kf[r, c] = block
        high, low = split(block)
        kh[r, c] = high
        kl[r, c] = low
    return 1.0 / (1.0 + jnp.sqrt(total))


def rotations(pairs, generator, works, out_high, out_low):
    part = [pl.ds(0, BLOCK), pl.ds(BLOCK, BLOCK)]
    upper = ((0, 0), (0, 1), (1, 1))
    held = [{} for _ in works]

    def turn(p):
        return p if len(works) == pairs else 0

    def start(p):
        c = generator(p, works[turn(p)])
        u = c * c
        b0, b1, b2, b3, b4 = POLY
        held[turn(p)]["c"] = c
        held[turn(p)]["k"] = (
            u,
            b0 + u * (b1 + u * (b2 + u * (b3 + u * b4))),
            b1 + u * (2 * b2 + u * (3 * b3 + u * 4 * b4)),
            b2 + u * (3 * b3 + u * 6 * b4),
            b3 + u * 4 * b4,
            b4,
        )

    def block(ah, al, bh, bl, i, j):
        r, c = part[i], part[j]
        return dot(ah[r, :], bh[:, c]) + (dot(ah[r, :], bl[:, c]) + dot(al[r, :], bh[:, c]))

    def put(high, low, i, j, value):
        high[part[i], part[j]], low[part[i], part[j]] = split(value)

    def put_symmetric(high, low, i, j, value):
        put(high, low, i, j, value)
        if i != j:
            put(high, low, j, i, value.T)

    def square(p):
        kf, kh, kl, sf, sh, sl, vf, vh, vl, th, tl, xh, xl, yh, yl = works[turn(p)]
        for i, j in upper:
            s = -held[turn(p)]["k"][0] * block(kh, kl, kh, kl, i, j)
            sf[part[i], part[j]] = s
            put_symmetric(sh, sl, i, j, s)

    def fourth(p):
        kf, kh, kl, sf, sh, sl, vf, vh, vl, th, tl, xh, xl, yh, yl = works[turn(p)]
        u, a0, a1, a2, a3, a4 = held[turn(p)]["k"]
        for i, j in upper:
            v = block(sh, sl, sh, sl, i, j)
            vf[part[i], part[j]] = v
            put_symmetric(vh, vl, i, j, v)
            put_symmetric(th, tl, i, j, a3 * sf[part[i], part[j]] + a4 * v)

    def polynomial(p):
        kf, kh, kl, sf, sh, sl, vf, vh, vl, th, tl, xh, xl, yh, yl = works[turn(p)]
        u, a0, a1, a2, a3, a4 = held[turn(p)]["k"]
        for i, j in upper:
            t = a1 * sf[part[i], part[j]] + a2 * vf[part[i], part[j]] + block(vh, vl, th, tl, i, j)
            vf[part[i], part[j]] = t
            put_symmetric(sh, sl, i, j, t)

    def second(p):
        kf, kh, kl, sf, sh, sl, vf, vh, vl, th, tl, xh, xl, yh, yl = works[turn(p)]
        u, a0, a1, a2, a3, a4 = held[turn(p)]["k"]
        c = held[turn(p)]["c"]
        for i, j in upper:
            odd = a0 * kf[part[i], part[j]] + block(kh, kl, sh, sl, i, j)
            even = vf[part[i], part[j]]
            if i == j:
                even = jnp.where(eye_mask(BLOCK), even + a0, even)
            x, y = c * (even - odd), c * (even + odd)
            sf[part[i], part[j]] = x
            put(xh, xl, i, j, x)
            put(yh, yl, i, j, y)
            if i != j:
                turned = y.T
                sf[part[j], part[i]] = turned
                put(xh, xl, j, i, turned)
                put(yh, yl, j, i, x.T)

    def metric(p):
        kf, kh, kl, sf, sh, sl, vf, vh, vl, th, tl, xh, xl, yh, yl = works[turn(p)]
        for i, j in upper:
            put_symmetric(vh, vl, i, j, block(yh, yl, xh, xl, i, j))

    def third(p):
        kf, kh, kl, sf, sh, sl, vf, vh, vl, th, tl, xh, xl, yh, yl = works[turn(p)]
        for cols in part:
            r = 1.5 * sf[:, cols] - 0.5 * product(xh, xl, vh, vl, cols)
            out_high[p, :, cols], out_low[p, :, cols] = split(r)

    stages = (start, square, fourth, polynomial, second, metric, third)
    if len(works) == pairs:
        for step in range(len(stages) + pairs - 1):
            for p in range(pairs):
                if 0 <= step - p < len(stages):
                    stages[step - p](p)
    else:

        @pl.loop(0, pairs)
        def _(p):
            for stage in stages:
                stage(p)


def leave(round_index, slots, src_ref, dev_ref, high_ref, low_ref, rh_ref, rl_ref, right_ref, left_ref):
    for step, out_ref in ((1, right_ref), (-1, left_ref)):
        slot = leaving(src_ref, dev_ref, round_index, step, slots)
        pair, half = slot >> 1, slot & 1
        rows = pl.ds(pl.multiple_of(pair * PAIR, PAIR), PAIR)
        cols = pl.ds(pl.multiple_of(half * BLOCK, BLOCK), BLOCK)
        out_ref[...] = product(
            high_ref.at[:, rows], low_ref.at[:, rows], rh_ref.at[pair], rl_ref.at[pair], cols
        )


def first_rotate(total_rows, slots, src_ref, dev_ref, sum_ref, high_ref, low_ref,
                 right_ref, left_ref, rh_ref, rl_ref, gh_ref, gl_ref, *rest):
    rows = sum_ref.shape[1] - 8
    per = BLOCK // rows
    works = [rest[at:at + 15] for at in range(0, len(rest), 15)]
    lo, hi = pl.ds(0, BLOCK), pl.ds(BLOCK, BLOCK)

    def generator(p, work):
        first_chunk = 2 * per * p
        cross = sum_ref[pl.ds(first_chunk, per), :rows, :].reshape(BLOCK, BLOCK)
        both = sum_ref[pl.ds(first_chunk + per, per), :rows, :].reshape(BLOCK, BLOCK)
        diagonal = sum_ref[first_chunk, rows:rows + 1, :]
        turned = both.T
        eye, upper = eye_mask(BLOCK), upper_mask(BLOCK)
        first = jnp.where(eye | upper, both, turned)
        second = jnp.where(eye, diagonal, jnp.where(upper, turned, both))
        for r, c, block in ((lo, lo, first), (lo, hi, cross), (hi, lo, cross.T), (hi, hi, second)):
            high, low = split(block)
            gh_ref[p, r, c] = high
            gl_ref[p, r, c] = low
        return set_generator(total_rows, cross, first, second, *work[:3])

    rotations(slots // 2, generator, works, rh_ref, rl_ref)
    leave(0, slots, src_ref, dev_ref, high_ref, low_ref, rh_ref, rl_ref, right_ref, left_ref)


def later_rotate(round_index, last, total_rows, slots, src_ref, dev_ref, sum_ref, self_ref,
                 high_ref, low_ref, right_ref, left_ref, rh_ref, rl_ref, *rest):
    rows = sum_ref.shape[1]
    per = BLOCK // rows
    if not last:
        gh_ref, gl_ref = rest[:2]
    rest = rest if last else rest[2:]
    works = [rest[at:at + 15] for at in range(0, len(rest), 15)]
    lo, hi = pl.ds(0, BLOCK), pl.ds(BLOCK, BLOCK)

    def generator(p, work):
        cross = sum_ref[pl.ds(p * per, per)].reshape(BLOCK, BLOCK)
        first, second = self_ref[2 * p], self_ref[2 * p + 1]
        if not last:
            for r, c, block in ((lo, lo, first), (lo, hi, cross), (hi, lo, cross.T), (hi, hi, second)):
                high, low = split(block)
                gh_ref[p, r, c] = high
                gl_ref[p, r, c] = low
        return set_generator(total_rows, cross, first, second, *work[:3])

    rotations(slots // 2, generator, works, rh_ref, rl_ref)
    leave(round_index, slots, src_ref, dev_ref, high_ref, low_ref, rh_ref, rl_ref, right_ref, left_ref)


def carry_self(round_index, slots, src_ref, dev_ref, gh_ref, gl_ref, rh_ref, rl_ref,
               self_ref, right_ref, left_ref, *work):
    @pl.loop(0, slots // 2)
    def _(p):
        for half in range(2):
            cols = pl.ds(half * BLOCK, BLOCK)
            yh, yl = work[2 * half:2 * half + 2]
            yh[...], yl[...] = split(product(gh_ref.at[p], gl_ref.at[p], rh_ref.at[p], rl_ref.at[p], cols))
        for half in range(2):
            cols = pl.ds(half * BLOCK, BLOCK)
            yh, yl = work[2 * half:2 * half + 2]
            self_ref[2 * p + half] = dot_t(rh_ref[p, :, cols], yh[...]) + (
                dot_t(rh_ref[p, :, cols], yl[...]) + dot_t(rl_ref[p, :, cols], yh[...])
            )

    right_ref[...] = self_ref[leaving(src_ref, dev_ref, round_index, 1, slots)]
    left_ref[...] = self_ref[leaving(src_ref, dev_ref, round_index, -1, slots)]


def take_self(round_index, slots, src_ref, dev_ref, self_ref, lower_ref, upper_ref, after_ref, out_ref):
    for slot in range(slots):
        offset = own_source(src_ref, dev_ref, round_index, slot, slots)
        out_ref[slot] = picked(offset, slots, self_ref, lower_ref, upper_ref)


def apply(slots, high_ref, low_ref, rh_ref, rl_ref, after_ref, own_ref):
    @pl.loop(0, slots // 2)
    def _(p):
        rows = pl.ds(pl.multiple_of(p * PAIR, PAIR), PAIR)
        for half in range(2):
            own_ref[2 * p + half] = product(
                high_ref.at[:, rows], low_ref.at[:, rows], rh_ref.at[p], rl_ref.at[p], pl.ds(half * BLOCK, BLOCK)
            )


def apply_last(round_index, slots, src_ref, dev_ref, high_ref, low_ref, rh_ref, rl_ref, out_ref, own_ref, sems):
    apply(slots, high_ref, low_ref, rh_ref, rl_ref, None, own_ref)
    offsets = [own_source(src_ref, dev_ref, round_index, slot, slots) for slot in range(slots)]
    for wait in (False, True):
        for slot, offset in enumerate(offsets):
            @pl.when((offset >= 0) & (offset < slots))
            def _():
                kept = own_ref.at[jnp.clip(offset, 0, slots - 1)]
                goal = out_ref.at[:, pl.ds(slot * BLOCK, BLOCK)]
                copy = pltpu.make_async_copy(kept, goal, sems.at[slot])
                copy.wait() if wait else copy.start()


def settle(round_index, slots, src_ref, dev_ref, most_ref, lower_ref, upper_ref, out_ref, sems):
    offsets = [own_source(src_ref, dev_ref, round_index, slot, slots) for slot in range(slots)]
    for wait in (False, True):
        for slot, offset in enumerate(offsets):
            goal = out_ref.at[:, pl.ds(slot * BLOCK, BLOCK)]

            @pl.when(offset < 0)
            def _():
                copy = pltpu.make_async_copy(lower_ref, goal, sems.at[slot])
                copy.wait() if wait else copy.start()

            @pl.when(offset >= slots)
            def _():
                copy = pltpu.make_async_copy(upper_ref, goal, sems.at[slot])
                copy.wait() if wait else copy.start()


def to_next(x, by):
    count = lax.axis_size("pair")
    return lax.ppermute(x, "pair", [(i, (i + by) % count) for i in range(count)])


def add_up(pieces_ref, out_ref):
    total = jnp.sum(pieces_ref[...], axis=0)
    for chunk in range(out_ref.shape[0]):
        out_ref[chunk] = total


def sum_rows(part):
    pieces = lax.all_to_all(part, "row", 0, 0, tiled=True)
    mine = call(add_up, jax.ShapeDtypeStruct(part.shape, F32), [VMEM])(pieces)
    return lax.all_to_all(mine, "row", 0, 0, tiled=True)


def body(matrix, sources):
    rows, columns = matrix.shape
    slots = columns // BLOCK
    pairs = slots // 2
    row_count = lax.axis_size("row")
    total_rows = rows * row_count
    device = lax.axis_index("pair").astype(jnp.int32).reshape(1)
    f32 = partial(jax.ShapeDtypeStruct, dtype=F32)
    bf16 = partial(jax.ShapeDtypeStruct, dtype=BF16)
    square = (PAIR, PAIR)
    f, h = pltpu.VMEM(square, F32), pltpu.VMEM(square, BF16)
    work = [f, h, h, f, h, h, f, h, h, h, h, h, h, h, h]
    product_flops = 2 * PAIR**3 * 3
    sems = pltpu.SemaphoreType.DMA((slots,))
    part, high, low = call(
        first_gram,
        (f32((row_count, 2 * slots * BLOCK // 2 // row_count + 8, BLOCK)), bf16(matrix.shape), bf16(matrix.shape)),
        [VMEM],
        flops=3 * pairs * product_flops // 4,
    )(matrix)
    part, sources, device = lax.optimization_barrier((part, sources, device))
    block, small = f32((rows, BLOCK)), f32((BLOCK, BLOCK))
    carried = ()
    for index in range(ROUNDS):
        last = index == ROUNDS - 1
        summed = sum_rows(part)
        kernel = first_rotate if index == 0 else partial(later_rotate, index, last)
        right, left, rh, rl, *gram = call(
            partial(kernel, total_rows, slots),
            (block, block) + (bf16((pairs,) + square),) * (2 if last else 4),
            [SMEM, SMEM] + [VMEM] * (3 + len(carried)),
            work * (pairs if index in UNROLLED else 1),
            flops=7 * pairs * product_flops,
            mib=20,
        )(sources, device, summed, *carried, high, low)
        lower, upper = to_next(right, 1), to_next(left, -1)
        if last:
            most = call(
                partial(apply_last, index, slots),
                f32(matrix.shape),
                [SMEM, SMEM] + [VMEM] * 4,
                [pltpu.VMEM((slots, rows, BLOCK), F32), sems],
                flops=pairs * product_flops,
                out_spec=ANY,
            )(sources, device, high, low, rh, rl)
            return call(
                partial(settle, index, slots),
                f32(matrix.shape),
                [SMEM, SMEM, ANY, VMEM, VMEM],
                [sems],
                out_spec=ANY,
                alias={2: 0},
            )(sources, device, most, lower, upper)
        selves, self_right, self_left = call(
            partial(carry_self, index, slots),
            (f32((slots, BLOCK, BLOCK)), small, small),
            [SMEM, SMEM] + [VMEM] * 4,
            [pltpu.VMEM((PAIR, BLOCK), BF16)] * 4,
            flops=3 * pairs * product_flops // 2,
        )(sources, device, *gram, rh, rl)
        own = call(
            partial(apply, slots),
            f32((slots, rows, BLOCK)),
            [VMEM] * 4 + [ANY],
            flops=pairs * product_flops,
        )(high, low, rh, rl, selves)
        lower_self, upper_self = to_next(self_right, 1), to_next(self_left, -1)
        part, high, low = call(
            partial(cross_gram, index, slots),
            (f32((row_count, pairs * BLOCK // row_count, BLOCK)), bf16(matrix.shape), bf16(matrix.shape)),
            [SMEM, SMEM] + [VMEM] * 3,
            flops=pairs * product_flops // 4,
        )(sources, device, own, lower, upper)
        selves = call(
            partial(take_self, index, slots), f32((slots, BLOCK, BLOCK)), [SMEM, SMEM] + [VMEM] * 3 + [ANY]
        )(sources, device, selves, lower_self, upper_self, part)
        part, *carried = lax.optimization_barrier((part, selves))


def solution(mesh):
    placed = (P("row", "pair"), P())
    return jax.shard_map(
        body, mesh=mesh, in_specs=placed, out_specs=P("row", "pair"), check_vma=False
    )
```

```python
from functools import partial

import jax
import jax.numpy as jnp
from jax import lax
from jax.experimental import pallas as pl
from jax.experimental.pallas import tpu as pltpu
from jax.sharding import PartitionSpec as P

BLOCK = 256
PAIR = 2 * BLOCK
LANES = 128
ROUNDS = 3
UNROLLED = (0, 1, 2)
F32 = jnp.float32
BF16 = jnp.bfloat16
POLY = (2.25, -2.4375, 1.6875, -0.5625, 0.0625)

VMEM = pl.BlockSpec(memory_space=pltpu.VMEM)
SMEM = pl.BlockSpec(memory_space=pltpu.SMEM)
ANY = pl.BlockSpec(memory_space=pl.ANY)


def call(kernel, out_shape, in_specs, scratch=(), flops=0, mib=10, out_spec=VMEM, alias=None):
    return pl.pallas_call(
        kernel,
        out_shape=out_shape,
        in_specs=in_specs,
        out_specs=jax.tree.map(lambda _: out_spec, out_shape),
        scratch_shapes=list(scratch),
        input_output_aliases=alias or {},
        compiler_params=pltpu.CompilerParams(vmem_limit_bytes=mib * 1024 * 1024),
        cost_estimate=pl.CostEstimate(flops=flops, bytes_accessed=4_000_000, transcendentals=0),
    )


def split(x):
    high = x.astype(BF16)
    return high, (x - high.astype(F32)).astype(BF16)


def dot(a, b):
    return jnp.dot(a, b, preferred_element_type=F32)


def dot_t(a, b):
    return lax.dot_general(a, b, (((0,), (0,)), ((), ())), preferred_element_type=F32)


def product(ah, al, bh, bl, cols, mul=dot):
    return mul(ah[...], bh[:, cols]) + (mul(ah[...], bl[:, cols]) + mul(al[...], bh[:, cols]))


def eye_mask(n):
    return lax.broadcasted_iota(jnp.int32, (n, n), 0) == lax.broadcasted_iota(jnp.int32, (n, n), 1)


def upper_mask(n):
    return lax.broadcasted_iota(jnp.int32, (n, n), 0) < lax.broadcasted_iota(jnp.int32, (n, n), 1)


def own_source(src_ref, dev_ref, round_index, slot, slots):
    base = dev_ref[0] * slots
    return src_ref[round_index, base + slot] - base


def leaving(src_ref, dev_ref, round_index, step, slots):
    base = dev_ref[0] * slots
    last = src_ref.shape[1] - slots
    there = jnp.clip(base + step * slots, 0, last)
    found = jnp.int32(0)
    for slot in range(slots):
        offset = src_ref[round_index, there + slot] - base
        found = jnp.where((offset >= 0) & (offset < slots), offset, found)
    return found


def picked(offset, slots, own_ref, lower_ref, upper_ref):
    own = own_ref[jnp.clip(offset, 0, slots - 1)]
    return jnp.where(offset < 0, lower_ref[...], jnp.where(offset >= slots, upper_ref[...], own))


def first_gram(a_ref, part_ref, high_ref, low_ref):
    pairs = a_ref.shape[1] // PAIR
    rows = (part_ref.shape[1] - 8) // 2
    per = BLOCK // rows
    part_ref[:, 2 * rows:, :] = jnp.zeros((part_ref.shape[0], 8, LANES), F32)
    for p in range(pairs):
        one, two = pl.ds(p * PAIR, BLOCK), pl.ds(p * PAIR + BLOCK, BLOCK)
        for cols in (one, two):
            high_ref[:, cols], low_ref[:, cols] = split(a_ref[:, cols])

        def gram(x, y):
            return dot_t(high_ref[:, x], high_ref[:, y]) + (
                dot_t(high_ref[:, x], low_ref[:, y]) + dot_t(low_ref[:, x], high_ref[:, y])
            )

        cross = gram(one, two)
        first = gram(one, one)
        second = gram(two, two)
        eye = eye_mask(BLOCK)
        diagonal = jnp.sum(jnp.where(eye, second, 0.0), axis=0, keepdims=True)
        both = jnp.where(eye | upper_mask(BLOCK), first, second)
        start = 2 * per * p
        for first_chunk, block in ((start, cross), (start + per, both)):
            for j in range(per):
                piece = block[j * rows:(j + 1) * rows]
                part_ref[first_chunk + j, :rows, :] = piece[:, :LANES]
                part_ref[first_chunk + j, rows:2 * rows, :] = piece[:, LANES:]
        part_ref[start, 2 * rows:2 * rows + 1, :] = diagonal[:, :LANES]
        part_ref[start, 2 * rows + 1:2 * rows + 2, :] = diagonal[:, LANES:]


def cross_gram(round_index, slots, src_ref, dev_ref, own_ref, lower_ref, upper_ref, part_ref, high_ref, low_ref):
    rows = part_ref.shape[1]
    per = BLOCK // rows
    for slot in range(slots):
        offset = own_source(src_ref, dev_ref, round_index, slot, slots)
        high, low = split(picked(offset, slots, own_ref, lower_ref, upper_ref))
        high_ref[:, pl.ds(slot * BLOCK, BLOCK)] = high
        low_ref[:, pl.ds(slot * BLOCK, BLOCK)] = low
    for p in range(slots // 2):
        one, two = pl.ds(p * PAIR, BLOCK), pl.ds(p * PAIR + BLOCK, BLOCK)
        cross = dot_t(high_ref[:, one], high_ref[:, two]) + (
            dot_t(high_ref[:, one], low_ref[:, two]) + dot_t(low_ref[:, one], high_ref[:, two])
        )
        for j in range(per):
            part_ref[p * per + j] = cross[j * rows:(j + 1) * rows]


def set_generator(total_rows, cross, first, second, kf, kh, kl):
    eye = eye_mask(BLOCK)
    sign = jnp.where(eye, 0.0, jnp.where(upper_mask(BLOCK), 1.0, -1.0))
    scale = 1.0 / total_rows
    roots = []
    for block in (first, second):
        kept = jnp.where(eye, block * scale, 0.0)
        roots.append(
            (
                lax.rsqrt(jnp.sum(kept, axis=1, keepdims=True) + 1e-06),
                lax.rsqrt(jnp.sum(kept, axis=0, keepdims=True) + 1e-06),
            )
        )
    k11 = first * scale * roots[0][0] * roots[0][1] * sign
    k22 = second * scale * roots[1][0] * roots[1][1] * sign
    k12 = cross * scale * roots[0][0] * roots[1][1]
    total = jnp.sum(k11 * k11 + k22 * k22 + 2.0 * (k12 * k12), keepdims=True)
    lo, hi = pl.ds(0, BLOCK), pl.ds(BLOCK, BLOCK)
    for r, c, block in ((lo, lo, k11), (lo, hi, k12), (hi, lo, -k12.T), (hi, hi, k22)):
        kf[r, c] = block
        high, low = split(block)
        kh[r, c] = high
        kl[r, c] = low
    return 1.0 / (1.0 + jnp.sqrt(total))


def rotations(pairs, generator, works, out_high, out_low):
    part = [pl.ds(0, BLOCK), pl.ds(BLOCK, BLOCK)]
    upper = ((0, 0), (0, 1), (1, 1))
    held = [{} for _ in works]

    def turn(p):
        return p if len(works) == pairs else 0

    def start(p):
        c = generator(p, works[turn(p)])
        u = c * c
        b0, b1, b2, b3, b4 = POLY
        held[turn(p)]["c"] = c
        held[turn(p)]["k"] = (
            u,
            b0 + u * (b1 + u * (b2 + u * (b3 + u * b4))),
            b1 + u * (2 * b2 + u * (3 * b3 + u * 4 * b4)),
            b2 + u * (3 * b3 + u * 6 * b4),
            b3 + u * 4 * b4,
            b4,
        )

    def block(ah, al, bh, bl, i, j):
        r, c = part[i], part[j]
        return dot(ah[r, :], bh[:, c]) + (dot(ah[r, :], bl[:, c]) + dot(al[r, :], bh[:, c]))

    def put(high, low, i, j, value):
        high[part[i], part[j]], low[part[i], part[j]] = split(value)

    def put_symmetric(high, low, i, j, value):
        put(high, low, i, j, value)
        if i != j:
            put(high, low, j, i, value.T)

    def square(p):
        kf, kh, kl, sf, sh, sl, vf, vh, vl, th, tl, xh, xl, yh, yl = works[turn(p)]
        for i, j in upper:
            s = -held[turn(p)]["k"][0] * block(kh, kl, kh, kl, i, j)
            sf[part[i], part[j]] = s
            put_symmetric(sh, sl, i, j, s)

    def fourth(p):
        kf, kh, kl, sf, sh, sl, vf, vh, vl, th, tl, xh, xl, yh, yl = works[turn(p)]
        u, a0, a1, a2, a3, a4 = held[turn(p)]["k"]
        for i, j in upper:
            v = block(sh, sl, sh, sl, i, j)
            vf[part[i], part[j]] = v
            put_symmetric(vh, vl, i, j, v)
            put_symmetric(th, tl, i, j, a3 * sf[part[i], part[j]] + a4 * v)

    def polynomial(p):
        kf, kh, kl, sf, sh, sl, vf, vh, vl, th, tl, xh, xl, yh, yl = works[turn(p)]
        u, a0, a1, a2, a3, a4 = held[turn(p)]["k"]
        for i, j in upper:
            t = a1 * sf[part[i], part[j]] + a2 * vf[part[i], part[j]] + block(vh, vl, th, tl, i, j)
            vf[part[i], part[j]] = t
            put_symmetric(sh, sl, i, j, t)

    def second(p):
        kf, kh, kl, sf, sh, sl, vf, vh, vl, th, tl, xh, xl, yh, yl = works[turn(p)]
        u, a0, a1, a2, a3, a4 = held[turn(p)]["k"]
        c = held[turn(p)]["c"]
        for i, j in upper:
            odd = a0 * kf[part[i], part[j]] + block(kh, kl, sh, sl, i, j)
            even = vf[part[i], part[j]]
            if i == j:
                even = jnp.where(eye_mask(BLOCK), even + a0, even)
            x, y = c * (even - odd), c * (even + odd)
            sf[part[i], part[j]] = x
            put(xh, xl, i, j, x)
            put(yh, yl, i, j, y)
            if i != j:
                turned = y.T
                sf[part[j], part[i]] = turned
                put(xh, xl, j, i, turned)
                put(yh, yl, j, i, x.T)

    def metric(p):
        kf, kh, kl, sf, sh, sl, vf, vh, vl, th, tl, xh, xl, yh, yl = works[turn(p)]
        for i, j in upper:
            put_symmetric(vh, vl, i, j, block(yh, yl, xh, xl, i, j))

    def third(p):
        kf, kh, kl, sf, sh, sl, vf, vh, vl, th, tl, xh, xl, yh, yl = works[turn(p)]
        for cols in part:
            r = 1.5 * sf[:, cols] - 0.5 * product(xh, xl, vh, vl, cols)
            out_high[p, :, cols], out_low[p, :, cols] = split(r)

    stages = (start, square, fourth, polynomial, second, metric, third)
    if len(works) == pairs:
        for step in range(len(stages) + pairs - 1):
            for p in range(pairs):
                if 0 <= step - p < len(stages):
                    stages[step - p](p)
    else:

        @pl.loop(0, pairs)
        def _(p):
            for stage in stages:
                stage(p)


def leave(round_index, slots, src_ref, dev_ref, high_ref, low_ref, rh_ref, rl_ref, right_ref, left_ref):
    for step, out_ref in ((1, right_ref), (-1, left_ref)):
        slot = leaving(src_ref, dev_ref, round_index, step, slots)
        pair, half = slot >> 1, slot & 1
        rows = pl.ds(pl.multiple_of(pair * PAIR, PAIR), PAIR)
        cols = pl.ds(pl.multiple_of(half * BLOCK, BLOCK), BLOCK)
        out_ref[...] = product(
            high_ref.at[:, rows], low_ref.at[:, rows], rh_ref.at[pair], rl_ref.at[pair], cols
        )


def first_rotate(total_rows, slots, src_ref, dev_ref, sum_ref, high_ref, low_ref,
                 right_ref, left_ref, rh_ref, rl_ref, gh_ref, gl_ref, *rest):
    rows = (sum_ref.shape[1] - 8) // 2
    per = BLOCK // rows
    works = [rest[at:at + 15] for at in range(0, len(rest), 15)]
    lo, hi = pl.ds(0, BLOCK), pl.ds(BLOCK, BLOCK)

    def generator(p, work):
        first_chunk = 2 * per * p

        def unpack(chunk):
            halves = [sum_ref[pl.ds(chunk, per), pl.ds(at, rows), :].reshape(BLOCK, LANES) for at in (0, rows)]
            return jnp.concatenate(halves, axis=1)

        cross, both = unpack(first_chunk), unpack(first_chunk + per)
        diagonal = jnp.concatenate([sum_ref[first_chunk, pl.ds(2 * rows + at, 1), :] for at in (0, 1)], axis=1)
        turned = both.T
        eye, upper = eye_mask(BLOCK), upper_mask(BLOCK)
        first = jnp.where(eye | upper, both, turned)
        second = jnp.where(eye, diagonal, jnp.where(upper, turned, both))
        for r, c, block in ((lo, lo, first), (lo, hi, cross), (hi, lo, cross.T), (hi, hi, second)):
            high, low = split(block)
            gh_ref[p, r, c] = high
            gl_ref[p, r, c] = low
        return set_generator(total_rows, cross, first, second, *work[:3])

    rotations(slots // 2, generator, works, rh_ref, rl_ref)
    leave(0, slots, src_ref, dev_ref, high_ref, low_ref, rh_ref, rl_ref, right_ref, left_ref)


def later_rotate(round_index, last, total_rows, slots, src_ref, dev_ref, sum_ref, self_ref,
                 high_ref, low_ref, right_ref, left_ref, rh_ref, rl_ref, *rest):
    rows = sum_ref.shape[1]
    per = BLOCK // rows
    if not last:
        gh_ref, gl_ref = rest[:2]
    rest = rest if last else rest[2:]
    works = [rest[at:at + 15] for at in range(0, len(rest), 15)]
    lo, hi = pl.ds(0, BLOCK), pl.ds(BLOCK, BLOCK)

    def generator(p, work):
        cross = sum_ref[pl.ds(p * per, per)].reshape(BLOCK, BLOCK)
        first, second = self_ref[2 * p], self_ref[2 * p + 1]
        if not last:
            for r, c, block in ((lo, lo, first), (lo, hi, cross), (hi, lo, cross.T), (hi, hi, second)):
                high, low = split(block)
                gh_ref[p, r, c] = high
                gl_ref[p, r, c] = low
        return set_generator(total_rows, cross, first, second, *work[:3])

    rotations(slots // 2, generator, works, rh_ref, rl_ref)
    leave(round_index, slots, src_ref, dev_ref, high_ref, low_ref, rh_ref, rl_ref, right_ref, left_ref)


def carry_self(round_index, slots, src_ref, dev_ref, gh_ref, gl_ref, rh_ref, rl_ref,
               self_ref, right_ref, left_ref, *work):
    @pl.loop(0, slots // 2)
    def _(p):
        for half in range(2):
            cols = pl.ds(half * BLOCK, BLOCK)
            yh, yl = work[2 * half:2 * half + 2]
            yh[...], yl[...] = split(product(gh_ref.at[p], gl_ref.at[p], rh_ref.at[p], rl_ref.at[p], cols))
        for half in range(2):
            cols = pl.ds(half * BLOCK, BLOCK)
            yh, yl = work[2 * half:2 * half + 2]
            self_ref[2 * p + half] = dot_t(rh_ref[p, :, cols], yh[...]) + (
                dot_t(rh_ref[p, :, cols], yl[...]) + dot_t(rl_ref[p, :, cols], yh[...])
            )

    right_ref[...] = self_ref[leaving(src_ref, dev_ref, round_index, 1, slots)]
    left_ref[...] = self_ref[leaving(src_ref, dev_ref, round_index, -1, slots)]


def apply(slots, high_ref, low_ref, rh_ref, rl_ref, after_ref, own_ref):
    @pl.loop(0, slots // 2)
    def _(p):
        rows = pl.ds(pl.multiple_of(p * PAIR, PAIR), PAIR)
        for half in range(2):
            own_ref[2 * p + half] = product(
                high_ref.at[:, rows], low_ref.at[:, rows], rh_ref.at[p], rl_ref.at[p], pl.ds(half * BLOCK, BLOCK)
            )


def apply_last(round_index, slots, src_ref, dev_ref, high_ref, low_ref, rh_ref, rl_ref, out_ref, own_ref, sems):
    apply(slots, high_ref, low_ref, rh_ref, rl_ref, None, own_ref)
    offsets = [own_source(src_ref, dev_ref, round_index, slot, slots) for slot in range(slots)]
    for wait in (False, True):
        for slot, offset in enumerate(offsets):
            @pl.when((offset >= 0) & (offset < slots))
            def _():
                kept = own_ref.at[jnp.clip(offset, 0, slots - 1)]
                goal = out_ref.at[:, pl.ds(slot * BLOCK, BLOCK)]
                copy = pltpu.make_async_copy(kept, goal, sems.at[slot])
                copy.wait() if wait else copy.start()


def settle(round_index, slots, src_ref, dev_ref, most_ref, lower_ref, upper_ref, out_ref, sems):
    offsets = [own_source(src_ref, dev_ref, round_index, slot, slots) for slot in range(slots)]
    for wait in (False, True):
        for slot, offset in enumerate(offsets):
            goal = out_ref.at[:, pl.ds(slot * BLOCK, BLOCK)]

            @pl.when(offset < 0)
            def _():
                copy = pltpu.make_async_copy(lower_ref, goal, sems.at[slot])
                copy.wait() if wait else copy.start()

            @pl.when(offset >= slots)
            def _():
                copy = pltpu.make_async_copy(upper_ref, goal, sems.at[slot])
                copy.wait() if wait else copy.start()


def to_next(x, by):
    count = lax.axis_size("pair")
    return lax.ppermute(x, "pair", [(i, (i + by) % count) for i in range(count)])


def add_up(pieces_ref, out_ref):
    total = jnp.sum(pieces_ref[...], axis=0)
    for chunk in range(out_ref.shape[0]):
        out_ref[chunk] = total


def add_up_and_take(round_index, slots, src_ref, dev_ref, pieces_ref, self_ref, lower_ref, upper_ref, out_ref, taken_ref):
    add_up(pieces_ref, out_ref)
    for slot in range(slots):
        offset = own_source(src_ref, dev_ref, round_index, slot, slots)
        taken_ref[slot] = picked(offset, slots, self_ref, lower_ref, upper_ref)


def from_rows(part):
    return lax.all_to_all(part, "row", 0, 0, tiled=True)


def body(matrix, sources):
    rows, columns = matrix.shape
    slots = columns // BLOCK
    pairs = slots // 2
    row_count = lax.axis_size("row")
    total_rows = rows * row_count
    device = lax.axis_index("pair").astype(jnp.int32).reshape(1)
    f32 = partial(jax.ShapeDtypeStruct, dtype=F32)
    bf16 = partial(jax.ShapeDtypeStruct, dtype=BF16)
    square = (PAIR, PAIR)
    f, h = pltpu.VMEM(square, F32), pltpu.VMEM(square, BF16)
    work = [f, h, h, f, h, h, f, h, h, h, h, h, h, h, h]
    product_flops = 2 * PAIR**3 * 3
    sems = pltpu.SemaphoreType.DMA((slots,))
    part, high, low = call(
        first_gram,
        (f32((row_count, BLOCK // LANES * slots * BLOCK // row_count + 8, LANES)), bf16(matrix.shape), bf16(matrix.shape)),
        [VMEM],
        flops=3 * pairs * product_flops // 4,
    )(matrix)
    part, sources, device = lax.optimization_barrier((part, sources, device))
    block, small = f32((rows, BLOCK)), f32((BLOCK, BLOCK))
    carried = ()
    summed = from_rows(call(add_up, f32(part.shape), [VMEM])(from_rows(part)))
    for index in range(ROUNDS):
        last = index == ROUNDS - 1
        kernel = first_rotate if index == 0 else partial(later_rotate, index, last)
        right, left, rh, rl, *gram = call(
            partial(kernel, total_rows, slots),
            (block, block) + (bf16((pairs,) + square),) * (2 if last else 4),
            [SMEM, SMEM] + [VMEM] * (3 + len(carried)),
            work * (pairs if index in UNROLLED else 1),
            flops=7 * pairs * product_flops,
            mib=20,
        )(sources, device, summed, *carried, high, low)
        lower, upper = to_next(right, 1), to_next(left, -1)
        if last:
            most = call(
                partial(apply_last, index, slots),
                f32(matrix.shape),
                [SMEM, SMEM] + [VMEM] * 4,
                [pltpu.VMEM((slots, rows, BLOCK), F32), sems],
                flops=pairs * product_flops,
                out_spec=ANY,
            )(sources, device, high, low, rh, rl)
            return call(
                partial(settle, index, slots),
                f32(matrix.shape),
                [SMEM, SMEM, ANY, VMEM, VMEM],
                [sems],
                out_spec=ANY,
                alias={2: 0},
            )(sources, device, most, lower, upper)
        selves, self_right, self_left = call(
            partial(carry_self, index, slots),
            (f32((slots, BLOCK, BLOCK)), small, small),
            [SMEM, SMEM] + [VMEM] * 4,
            [pltpu.VMEM((PAIR, BLOCK), BF16)] * 4,
            flops=3 * pairs * product_flops // 2,
        )(sources, device, *gram, rh, rl)
        own = call(
            partial(apply, slots),
            f32((slots, rows, BLOCK)),
            [VMEM] * 4 + [ANY],
            flops=pairs * product_flops,
        )(high, low, rh, rl, selves)
        lower_self, upper_self = to_next(self_right, 1), to_next(self_left, -1)
        part, high, low = call(
            partial(cross_gram, index, slots),
            (f32((row_count, pairs * BLOCK // row_count, BLOCK)), bf16(matrix.shape), bf16(matrix.shape)),
            [SMEM, SMEM] + [VMEM] * 3,
            flops=pairs * product_flops // 4,
        )(sources, device, own, lower, upper)
        part, lower_self, upper_self = lax.optimization_barrier((part, lower_self, upper_self))
        mine, selves = call(
            partial(add_up_and_take, index, slots),
            (f32(part.shape), f32((slots, BLOCK, BLOCK))),
            [SMEM, SMEM] + [VMEM] * 4,
        )(sources, device, from_rows(part), selves, lower_self, upper_self)
        carried = (selves,)
        summed = from_rows(mine)


def solution(mesh):
    placed = (P("row", "pair"), P())
    return jax.shard_map(
        body, mesh=mesh, in_specs=placed, out_specs=P("row", "pair"), check_vma=False
    )
```

```python
from functools import partial

import jax
import jax.numpy as jnp
from jax import lax
from jax.experimental import pallas as pl
from jax.experimental.pallas import tpu as pltpu
from jax.sharding import PartitionSpec as P

BLOCK = 256
PAIR = 2 * BLOCK
LANES = 128
ROUNDS = 3
UNROLLED = (0, 1, 2)
F32 = jnp.float32
BF16 = jnp.bfloat16
POLY = (2.25, -2.4375, 1.6875, -0.5625, 0.0625)

VMEM = pl.BlockSpec(memory_space=pltpu.VMEM)
SMEM = pl.BlockSpec(memory_space=pltpu.SMEM)
ANY = pl.BlockSpec(memory_space=pl.ANY)


def call(kernel, out_shape, in_specs, scratch=(), flops=0, mib=10, out_spec=VMEM, alias=None):
    return pl.pallas_call(
        kernel,
        out_shape=out_shape,
        in_specs=in_specs,
        out_specs=jax.tree.map(lambda _: out_spec, out_shape),
        scratch_shapes=list(scratch),
        input_output_aliases=alias or {},
        compiler_params=pltpu.CompilerParams(vmem_limit_bytes=mib * 1024 * 1024),
        cost_estimate=pl.CostEstimate(flops=flops, bytes_accessed=4_000_000, transcendentals=0),
    )


def split(x):
    high = x.astype(BF16)
    return high, (x - high.astype(F32)).astype(BF16)


def dot(a, b):
    return jnp.dot(a, b, preferred_element_type=F32)


def dot_t(a, b):
    return lax.dot_general(a, b, (((0,), (0,)), ((), ())), preferred_element_type=F32)


def product(ah, al, bh, bl, cols, mul=dot):
    return mul(ah[...], bh[:, cols]) + (mul(ah[...], bl[:, cols]) + mul(al[...], bh[:, cols]))


def eye_mask(n):
    return lax.broadcasted_iota(jnp.int32, (n, n), 0) == lax.broadcasted_iota(jnp.int32, (n, n), 1)


def upper_mask(n):
    return lax.broadcasted_iota(jnp.int32, (n, n), 0) < lax.broadcasted_iota(jnp.int32, (n, n), 1)


def own_source(src_ref, round_index, slot, slots):
    base = lax.axis_index("pair") * slots
    return src_ref[round_index, base + slot] - base


def leaving(src_ref, round_index, step, slots):
    base = lax.axis_index("pair") * slots
    last = src_ref.shape[1] - slots
    there = jnp.clip(base + step * slots, 0, last)
    found = jnp.int32(0)
    for slot in range(slots):
        offset = src_ref[round_index, there + slot] - base
        found = jnp.where((offset >= 0) & (offset < slots), offset, found)
    return found


def picked(offset, slots, own_ref, lower_ref, upper_ref):
    own = own_ref[jnp.clip(offset, 0, slots - 1)]
    return jnp.where(offset < 0, lower_ref[...], jnp.where(offset >= slots, upper_ref[...], own))


def first_gram(a_ref, part_ref, high_ref, low_ref):
    pairs = a_ref.shape[1] // PAIR
    rows = (part_ref.shape[1] - 8) // 2
    per = BLOCK // rows
    part_ref[:, 2 * rows:, :] = jnp.zeros((part_ref.shape[0], 8, LANES), F32)
    for p in range(pairs):
        one, two = pl.ds(p * PAIR, BLOCK), pl.ds(p * PAIR + BLOCK, BLOCK)
        for cols in (one, two):
            high_ref[:, cols], low_ref[:, cols] = split(a_ref[:, cols])

        def gram(x, y):
            return dot_t(high_ref[:, x], high_ref[:, y]) + (
                dot_t(high_ref[:, x], low_ref[:, y]) + dot_t(low_ref[:, x], high_ref[:, y])
            )

        cross = gram(one, two)
        first = gram(one, one)
        second = gram(two, two)
        eye = eye_mask(BLOCK)
        diagonal = jnp.sum(jnp.where(eye, second, 0.0), axis=0, keepdims=True)
        both = jnp.where(eye | upper_mask(BLOCK), first, second)
        start = 2 * per * p
        for first_chunk, block in ((start, cross), (start + per, both)):
            for j in range(per):
                piece = block[j * rows:(j + 1) * rows]
                part_ref[first_chunk + j, :rows, :] = piece[:, :LANES]
                part_ref[first_chunk + j, rows:2 * rows, :] = piece[:, LANES:]
        part_ref[start, 2 * rows:2 * rows + 1, :] = diagonal[:, :LANES]
        part_ref[start, 2 * rows + 1:2 * rows + 2, :] = diagonal[:, LANES:]


def cross_gram(round_index, slots, src_ref, own_ref, lower_ref, upper_ref, part_ref, high_ref, low_ref):
    rows = part_ref.shape[1]
    per = BLOCK // rows
    for slot in range(slots):
        offset = own_source(src_ref, round_index, slot, slots)
        high, low = split(picked(offset, slots, own_ref, lower_ref, upper_ref))
        high_ref[:, pl.ds(slot * BLOCK, BLOCK)] = high
        low_ref[:, pl.ds(slot * BLOCK, BLOCK)] = low
    for p in range(slots // 2):
        one, two = pl.ds(p * PAIR, BLOCK), pl.ds(p * PAIR + BLOCK, BLOCK)
        cross = dot_t(high_ref[:, one], high_ref[:, two]) + (
            dot_t(high_ref[:, one], low_ref[:, two]) + dot_t(low_ref[:, one], high_ref[:, two])
        )
        for j in range(per):
            part_ref[p * per + j] = cross[j * rows:(j + 1) * rows]


def set_generator(total_rows, cross, first, second, kf, kh, kl):
    eye = eye_mask(BLOCK)
    sign = jnp.where(eye, 0.0, jnp.where(upper_mask(BLOCK), 1.0, -1.0))
    scale = 1.0 / total_rows
    roots = []
    for block in (first, second):
        kept = jnp.where(eye, block * scale, 0.0)
        roots.append(
            (
                lax.rsqrt(jnp.sum(kept, axis=1, keepdims=True) + 1e-06),
                lax.rsqrt(jnp.sum(kept, axis=0, keepdims=True) + 1e-06),
            )
        )
    k11 = first * scale * roots[0][0] * roots[0][1] * sign
    k22 = second * scale * roots[1][0] * roots[1][1] * sign
    k12 = cross * scale * roots[0][0] * roots[1][1]
    total = jnp.sum(k11 * k11 + k22 * k22 + 2.0 * (k12 * k12), keepdims=True)
    lo, hi = pl.ds(0, BLOCK), pl.ds(BLOCK, BLOCK)
    for r, c, block in ((lo, lo, k11), (lo, hi, k12), (hi, lo, -k12.T), (hi, hi, k22)):
        kf[r, c] = block
        high, low = split(block)
        kh[r, c] = high
        kl[r, c] = low
    return 1.0 / (1.0 + jnp.sqrt(total))


def rotations(pairs, generator, works, out_high, out_low):
    part = [pl.ds(0, BLOCK), pl.ds(BLOCK, BLOCK)]
    upper = ((0, 0), (0, 1), (1, 1))
    held = [{} for _ in works]

    def turn(p):
        return p if len(works) == pairs else 0

    def start(p):
        c = generator(p, works[turn(p)])
        u = c * c
        b0, b1, b2, b3, b4 = POLY
        held[turn(p)]["c"] = c
        held[turn(p)]["k"] = (
            u,
            b0 + u * (b1 + u * (b2 + u * (b3 + u * b4))),
            b1 + u * (2 * b2 + u * (3 * b3 + u * 4 * b4)),
            b2 + u * (3 * b3 + u * 6 * b4),
            b3 + u * 4 * b4,
            b4,
        )

    def block(ah, al, bh, bl, i, j):
        r, c = part[i], part[j]
        return dot(ah[r, :], bh[:, c]) + (dot(ah[r, :], bl[:, c]) + dot(al[r, :], bh[:, c]))

    def put(high, low, i, j, value):
        high[part[i], part[j]], low[part[i], part[j]] = split(value)

    def put_symmetric(high, low, i, j, value):
        put(high, low, i, j, value)
        if i != j:
            put(high, low, j, i, value.T)

    def square(p):
        kf, kh, kl, sf, sh, sl, vf, vh, vl, th, tl, xh, xl, yh, yl = works[turn(p)]
        for i, j in upper:
            s = -held[turn(p)]["k"][0] * block(kh, kl, kh, kl, i, j)
            sf[part[i], part[j]] = s
            put_symmetric(sh, sl, i, j, s)

    def fourth(p):
        kf, kh, kl, sf, sh, sl, vf, vh, vl, th, tl, xh, xl, yh, yl = works[turn(p)]
        u, a0, a1, a2, a3, a4 = held[turn(p)]["k"]
        for i, j in upper:
            v = block(sh, sl, sh, sl, i, j)
            vf[part[i], part[j]] = v
            put_symmetric(vh, vl, i, j, v)
            put_symmetric(th, tl, i, j, a3 * sf[part[i], part[j]] + a4 * v)

    def polynomial(p):
        kf, kh, kl, sf, sh, sl, vf, vh, vl, th, tl, xh, xl, yh, yl = works[turn(p)]
        u, a0, a1, a2, a3, a4 = held[turn(p)]["k"]
        for i, j in upper:
            t = a1 * sf[part[i], part[j]] + a2 * vf[part[i], part[j]] + block(vh, vl, th, tl, i, j)
            vf[part[i], part[j]] = t
            put_symmetric(sh, sl, i, j, t)

    def second(p):
        kf, kh, kl, sf, sh, sl, vf, vh, vl, th, tl, xh, xl, yh, yl = works[turn(p)]
        u, a0, a1, a2, a3, a4 = held[turn(p)]["k"]
        c = held[turn(p)]["c"]
        for i, j in upper:
            odd = a0 * kf[part[i], part[j]] + block(kh, kl, sh, sl, i, j)
            even = vf[part[i], part[j]]
            if i == j:
                even = jnp.where(eye_mask(BLOCK), even + a0, even)
            x, y = c * (even - odd), c * (even + odd)
            sf[part[i], part[j]] = x
            put(xh, xl, i, j, x)
            put(yh, yl, i, j, y)
            if i != j:
                turned = y.T
                sf[part[j], part[i]] = turned
                put(xh, xl, j, i, turned)
                put(yh, yl, j, i, x.T)

    def metric(p):
        kf, kh, kl, sf, sh, sl, vf, vh, vl, th, tl, xh, xl, yh, yl = works[turn(p)]
        for i, j in upper:
            put_symmetric(vh, vl, i, j, block(yh, yl, xh, xl, i, j))

    def third(p):
        kf, kh, kl, sf, sh, sl, vf, vh, vl, th, tl, xh, xl, yh, yl = works[turn(p)]
        for cols in part:
            r = 1.5 * sf[:, cols] - 0.5 * product(xh, xl, vh, vl, cols)
            out_high[p, :, cols], out_low[p, :, cols] = split(r)

    stages = (start, square, fourth, polynomial, second, metric, third)
    if len(works) == pairs:
        for step in range(len(stages) + pairs - 1):
            for p in range(pairs):
                if 0 <= step - p < len(stages):
                    stages[step - p](p)
    else:

        @pl.loop(0, pairs)
        def _(p):
            for stage in stages:
                stage(p)


def fetch(table_ref, held, sem):
    copy = pltpu.make_async_copy(table_ref, held, sem)
    copy.start()
    return copy


def leave(round_index, slots, src_ref, high_ref, low_ref, rh_ref, rl_ref, right_ref, left_ref):
    for step, out_ref in ((1, right_ref), (-1, left_ref)):
        slot = leaving(src_ref, round_index, step, slots)
        pair, half = slot >> 1, slot & 1
        rows = pl.ds(pl.multiple_of(pair * PAIR, PAIR), PAIR)
        cols = pl.ds(pl.multiple_of(half * BLOCK, BLOCK), BLOCK)
        out_ref[...] = product(
            high_ref.at[:, rows], low_ref.at[:, rows], rh_ref.at[pair], rl_ref.at[pair], cols
        )


def first_rotate(total_rows, slots, table_ref, sum_ref, high_ref, low_ref,
                 right_ref, left_ref, rh_ref, rl_ref, gh_ref, gl_ref, src_ref, sem, *rest):
    table = fetch(table_ref, src_ref, sem)
    rows = (sum_ref.shape[1] - 8) // 2
    per = BLOCK // rows
    works = [rest[at:at + 15] for at in range(0, len(rest), 15)]
    lo, hi = pl.ds(0, BLOCK), pl.ds(BLOCK, BLOCK)

    def generator(p, work):
        first_chunk = 2 * per * p

        def unpack(chunk):
            halves = [sum_ref[pl.ds(chunk, per), pl.ds(at, rows), :].reshape(BLOCK, LANES) for at in (0, rows)]
            return jnp.concatenate(halves, axis=1)

        cross, both = unpack(first_chunk), unpack(first_chunk + per)
        diagonal = jnp.concatenate([sum_ref[first_chunk, pl.ds(2 * rows + at, 1), :] for at in (0, 1)], axis=1)
        turned = both.T
        eye, upper = eye_mask(BLOCK), upper_mask(BLOCK)
        first = jnp.where(eye | upper, both, turned)
        second = jnp.where(eye, diagonal, jnp.where(upper, turned, both))
        for r, c, block in ((lo, lo, first), (lo, hi, cross), (hi, lo, cross.T), (hi, hi, second)):
            high, low = split(block)
            gh_ref[p, r, c] = high
            gl_ref[p, r, c] = low
        return set_generator(total_rows, cross, first, second, *work[:3])

    rotations(slots // 2, generator, works, rh_ref, rl_ref)
    table.wait()
    leave(0, slots, src_ref, high_ref, low_ref, rh_ref, rl_ref, right_ref, left_ref)


def later_rotate(round_index, last, total_rows, slots, table_ref, sum_ref, self_ref,
                 high_ref, low_ref, right_ref, left_ref, rh_ref, rl_ref, *rest):
    rows = sum_ref.shape[1]
    per = BLOCK // rows
    if not last:
        gh_ref, gl_ref = rest[:2]
    src_ref, sem, *rest = rest if last else rest[2:]
    table = fetch(table_ref, src_ref, sem)
    works = [rest[at:at + 15] for at in range(0, len(rest), 15)]
    lo, hi = pl.ds(0, BLOCK), pl.ds(BLOCK, BLOCK)

    def generator(p, work):
        cross = sum_ref[pl.ds(p * per, per)].reshape(BLOCK, BLOCK)
        first, second = self_ref[2 * p], self_ref[2 * p + 1]
        if not last:
            for r, c, block in ((lo, lo, first), (lo, hi, cross), (hi, lo, cross.T), (hi, hi, second)):
                high, low = split(block)
                gh_ref[p, r, c] = high
                gl_ref[p, r, c] = low
        return set_generator(total_rows, cross, first, second, *work[:3])

    rotations(slots // 2, generator, works, rh_ref, rl_ref)
    table.wait()
    leave(round_index, slots, src_ref, high_ref, low_ref, rh_ref, rl_ref, right_ref, left_ref)


def carry_self(round_index, slots, table_ref, gh_ref, gl_ref, rh_ref, rl_ref,
               self_ref, right_ref, left_ref, src_ref, sem, *work):
    table = fetch(table_ref, src_ref, sem)
    @pl.loop(0, slots // 2)
    def _(p):
        for half in range(2):
            cols = pl.ds(half * BLOCK, BLOCK)
            yh, yl = work[2 * half:2 * half + 2]
            yh[...], yl[...] = split(product(gh_ref.at[p], gl_ref.at[p], rh_ref.at[p], rl_ref.at[p], cols))
        for half in range(2):
            cols = pl.ds(half * BLOCK, BLOCK)
            yh, yl = work[2 * half:2 * half + 2]
            self_ref[2 * p + half] = dot_t(rh_ref[p, :, cols], yh[...]) + (
                dot_t(rh_ref[p, :, cols], yl[...]) + dot_t(rl_ref[p, :, cols], yh[...])
            )

    table.wait()
    for step, out_ref in ((1, right_ref), (-1, left_ref)):
        slot = leaving(src_ref, round_index, step, slots)
        out_ref[:LANES, :] = self_ref[slot, :LANES, :]
        for half in range(2):
            rows = pl.ds(LANES + half * LANES // 2, LANES // 2)
            out_ref[LANES:, pl.ds(half * LANES, LANES)] = self_ref[slot, rows, LANES:]


def apply(slots, high_ref, low_ref, rh_ref, rl_ref, after_ref, own_ref):
    @pl.loop(0, slots // 2)
    def _(p):
        rows = pl.ds(pl.multiple_of(p * PAIR, PAIR), PAIR)
        for half in range(2):
            own_ref[2 * p + half] = product(
                high_ref.at[:, rows], low_ref.at[:, rows], rh_ref.at[p], rl_ref.at[p], pl.ds(half * BLOCK, BLOCK)
            )


def apply_last(round_index, slots, table_ref, high_ref, low_ref, rh_ref, rl_ref, out_ref, src_ref, sem, own_ref, sems):
    table = fetch(table_ref, src_ref, sem)
    apply(slots, high_ref, low_ref, rh_ref, rl_ref, None, own_ref)
    table.wait()
    offsets = [own_source(src_ref, round_index, slot, slots) for slot in range(slots)]
    for wait in (False, True):
        for slot, offset in enumerate(offsets):
            @pl.when((offset >= 0) & (offset < slots))
            def _():
                kept = own_ref.at[jnp.clip(offset, 0, slots - 1)]
                goal = out_ref.at[:, pl.ds(slot * BLOCK, BLOCK)]
                copy = pltpu.make_async_copy(kept, goal, sems.at[slot])
                copy.wait() if wait else copy.start()


def settle(round_index, slots, src_ref, most_ref, lower_ref, upper_ref, out_ref, sems):
    offsets = [own_source(src_ref, round_index, slot, slots) for slot in range(slots)]
    for wait in (False, True):
        for slot, offset in enumerate(offsets):
            goal = out_ref.at[:, pl.ds(slot * BLOCK, BLOCK)]

            @pl.when(offset < 0)
            def _():
                copy = pltpu.make_async_copy(lower_ref, goal, sems.at[slot])
                copy.wait() if wait else copy.start()

            @pl.when(offset >= slots)
            def _():
                copy = pltpu.make_async_copy(upper_ref, goal, sems.at[slot])
                copy.wait() if wait else copy.start()


def to_next(x, by):
    count = lax.axis_size("pair")
    return lax.ppermute(x, "pair", [(i, (i + by) % count) for i in range(count)])


def add_up(pieces_ref, out_ref):
    total = jnp.sum(pieces_ref[...], axis=0)
    for chunk in range(out_ref.shape[0]):
        out_ref[chunk] = total


def add_up_and_take(round_index, slots, table_ref, pieces_ref, self_ref, lower_ref, upper_ref,
                    out_ref, taken_ref, src_ref, sem, lower_full, upper_full):
    table = fetch(table_ref, src_ref, sem)
    add_up(pieces_ref, out_ref)
    for packed, full in ((lower_ref, lower_full), (upper_ref, upper_full)):
        full[:LANES, :] = packed[:LANES, :]
        full[LANES:, :LANES] = packed[:LANES, LANES:].T
        for half in range(2):
            rows = pl.ds(LANES + half * LANES // 2, LANES // 2)
            full[rows, LANES:] = packed[LANES:, pl.ds(half * LANES, LANES)]
    table.wait()
    for slot in range(slots):
        offset = own_source(src_ref, round_index, slot, slots)
        taken_ref[slot] = picked(offset, slots, self_ref, lower_full, upper_full)


def from_rows(part):
    return lax.all_to_all(part, "row", 0, 0, tiled=True)


def body(matrix, sources):
    rows, columns = matrix.shape
    slots = columns // BLOCK
    pairs = slots // 2
    row_count = lax.axis_size("row")
    total_rows = rows * row_count
    f32 = partial(jax.ShapeDtypeStruct, dtype=F32)
    bf16 = partial(jax.ShapeDtypeStruct, dtype=BF16)
    square = (PAIR, PAIR)
    f, h = pltpu.VMEM(square, F32), pltpu.VMEM(square, BF16)
    work = [f, h, h, f, h, h, f, h, h, h, h, h, h, h, h]
    product_flops = 2 * PAIR**3 * 3
    sems = pltpu.SemaphoreType.DMA((slots,))
    part, high, low = call(
        first_gram,
        (f32((row_count, BLOCK // LANES * slots * BLOCK // row_count + 8, LANES)), bf16(matrix.shape), bf16(matrix.shape)),
        [VMEM],
        flops=3 * pairs * product_flops // 4,
    )(matrix)
    part, sources = lax.optimization_barrier((part, sources))
    block, small = f32((rows, BLOCK)), f32((BLOCK * 3 // 4, BLOCK))
    table = [pltpu.SMEM(sources.shape, jnp.int32), pltpu.SemaphoreType.DMA]
    carried = ()
    summed = from_rows(call(add_up, f32(part.shape), [VMEM])(from_rows(part)))
    for index in range(ROUNDS):
        last = index == ROUNDS - 1
        kernel = first_rotate if index == 0 else partial(later_rotate, index, last)
        right, left, rh, rl, *gram = call(
            partial(kernel, total_rows, slots),
            (block, block) + (bf16((pairs,) + square),) * (2 if last else 4),
            [ANY] + [VMEM] * (3 + len(carried)),
            table + work * (pairs if index in UNROLLED else 1),
            flops=7 * pairs * product_flops,
            mib=20,
        )(sources, summed, *carried, high, low)
        lower, upper = to_next(right, 1), to_next(left, -1)
        if last:
            most = call(
                partial(apply_last, index, slots),
                f32(matrix.shape),
                [ANY] + [VMEM] * 4,
                table + [pltpu.VMEM((slots, rows, BLOCK), F32), sems],
                flops=pairs * product_flops,
                out_spec=ANY,
            )(sources, high, low, rh, rl)
            return call(
                partial(settle, index, slots),
                f32(matrix.shape),
                [SMEM, ANY, VMEM, VMEM],
                [sems],
                out_spec=ANY,
                alias={1: 0},
            )(sources, most, lower, upper)
        selves, self_right, self_left = call(
            partial(carry_self, index, slots),
            (f32((slots, BLOCK, BLOCK)), small, small),
            [ANY] + [VMEM] * 4,
            table + [pltpu.VMEM((PAIR, BLOCK), BF16)] * 4,
            flops=3 * pairs * product_flops // 2,
        )(sources, *gram, rh, rl)
        own = call(
            partial(apply, slots),
            f32((slots, rows, BLOCK)),
            [VMEM] * 4 + [ANY],
            flops=pairs * product_flops,
        )(high, low, rh, rl, selves)
        lower_self, upper_self = to_next(self_right, 1), to_next(self_left, -1)
        part, high, low = call(
            partial(cross_gram, index, slots),
            (f32((row_count, pairs * BLOCK // row_count, BLOCK)), bf16(matrix.shape), bf16(matrix.shape)),
            [SMEM] + [VMEM] * 3,
            flops=pairs * product_flops // 4,
        )(sources, own, lower, upper)
        part, lower_self, upper_self = lax.optimization_barrier((part, lower_self, upper_self))
        mine, selves = call(
            partial(add_up_and_take, index, slots),
            (f32(part.shape), f32((slots, BLOCK, BLOCK))),
            [ANY] + [VMEM] * 4,
            table + [pltpu.VMEM((BLOCK, BLOCK), F32)] * 2,
        )(sources, from_rows(part), selves, lower_self, upper_self)
        carried = (selves,)
        summed = from_rows(mine)


def solution(mesh):
    placed = (P("row", "pair"), P())
    return jax.shard_map(
        body, mesh=mesh, in_specs=placed, out_specs=P("row", "pair"), check_vma=False
    )
```

```python
from functools import partial

import jax
import jax.numpy as jnp
from jax import lax
from jax.experimental import pallas as pl
from jax.experimental.pallas import tpu as pltpu
from jax.sharding import PartitionSpec as P

BLOCK = 256
PAIR = 2 * BLOCK
LANES = 128
ROUNDS = 3
UNROLLED = (0, 1, 2)
F32 = jnp.float32
BF16 = jnp.bfloat16
POLY = (2.25, -2.4375, 1.6875, -0.5625, 0.0625)

VMEM = pl.BlockSpec(memory_space=pltpu.VMEM)
ANY = pl.BlockSpec(memory_space=pl.ANY)


def call(kernel, out_shape, in_specs, scratch=(), flops=0, mib=10, out_spec=VMEM, alias=None):
    return pl.pallas_call(
        kernel,
        out_shape=out_shape,
        in_specs=in_specs,
        out_specs=jax.tree.map(lambda _: out_spec, out_shape),
        scratch_shapes=list(scratch),
        input_output_aliases=alias or {},
        compiler_params=pltpu.CompilerParams(vmem_limit_bytes=mib * 1024 * 1024),
        cost_estimate=pl.CostEstimate(flops=flops, bytes_accessed=4_000_000, transcendentals=0),
    )


def split(x):
    high = x.astype(BF16)
    return high, (x - high.astype(F32)).astype(BF16)


def dot(a, b):
    return jnp.dot(a, b, preferred_element_type=F32)


def dot_t(a, b):
    return lax.dot_general(a, b, (((0,), (0,)), ((), ())), preferred_element_type=F32)


def product(ah, al, bh, bl, cols, mul=dot):
    return mul(ah[...], bh[:, cols]) + (mul(ah[...], bl[:, cols]) + mul(al[...], bh[:, cols]))


def eye_mask(n):
    return lax.broadcasted_iota(jnp.int32, (n, n), 0) == lax.broadcasted_iota(jnp.int32, (n, n), 1)


def upper_mask(n):
    return lax.broadcasted_iota(jnp.int32, (n, n), 0) < lax.broadcasted_iota(jnp.int32, (n, n), 1)


def own_source(src_ref, round_index, slot, slots):
    base = lax.axis_index("pair") * slots
    return src_ref[round_index, base + slot] - base


def own_sources(table_ref, round_index, slots):
    base = lax.axis_index("pair") * slots
    row = table_ref[pl.ds(round_index, 1), :].astype(F32)
    lane = lax.broadcasted_iota(jnp.int32, row.shape, 1)
    return [jnp.sum(jnp.where(lane == base + slot, row, 0.0)).astype(jnp.int32) - base for slot in range(slots)]


def leaving(src_ref, round_index, step, slots):
    base = lax.axis_index("pair") * slots
    last = src_ref.shape[1] - slots
    there = jnp.clip(base + step * slots, 0, last)
    found = jnp.int32(0)
    for slot in range(slots):
        offset = src_ref[round_index, there + slot] - base
        found = jnp.where((offset >= 0) & (offset < slots), offset, found)
    return found


def picked(offset, slots, own_ref, lower_ref, upper_ref):
    own = own_ref[jnp.clip(offset, 0, slots - 1)]
    return jnp.where(offset < 0, lower_ref[...], jnp.where(offset >= slots, upper_ref[...], own))


def first_gram(a_ref, part_ref, high_ref, low_ref):
    pairs = a_ref.shape[1] // PAIR
    rows = (part_ref.shape[1] - 8) // 2
    per = BLOCK // rows
    part_ref[:, 2 * rows:, :] = jnp.zeros((part_ref.shape[0], 8, LANES), F32)
    for p in range(pairs):
        one, two = pl.ds(p * PAIR, BLOCK), pl.ds(p * PAIR + BLOCK, BLOCK)
        for cols in (one, two):
            high_ref[:, cols], low_ref[:, cols] = split(a_ref[:, cols])

        def gram(x, y):
            return dot_t(high_ref[:, x], high_ref[:, y]) + (
                dot_t(high_ref[:, x], low_ref[:, y]) + dot_t(low_ref[:, x], high_ref[:, y])
            )

        cross = gram(one, two)
        first = gram(one, one)
        second = gram(two, two)
        eye = eye_mask(BLOCK)
        diagonal = jnp.sum(jnp.where(eye, second, 0.0), axis=0, keepdims=True)
        both = jnp.where(eye | upper_mask(BLOCK), first, second)
        start = 2 * per * p
        for first_chunk, block in ((start, cross), (start + per, both)):
            for j in range(per):
                piece = block[j * rows:(j + 1) * rows]
                part_ref[first_chunk + j, :rows, :] = piece[:, :LANES]
                part_ref[first_chunk + j, rows:2 * rows, :] = piece[:, LANES:]
        part_ref[start, 2 * rows:2 * rows + 1, :] = diagonal[:, :LANES]
        part_ref[start, 2 * rows + 1:2 * rows + 2, :] = diagonal[:, LANES:]


def cross_gram(round_index, slots, src_ref, own_ref, lower_ref, upper_ref, part_ref, high_ref, low_ref):
    rows = part_ref.shape[1]
    per = BLOCK // rows
    for slot, offset in enumerate(own_sources(src_ref, round_index, slots)):
        high, low = split(picked(offset, slots, own_ref, lower_ref, upper_ref))
        high_ref[:, pl.ds(slot * BLOCK, BLOCK)] = high
        low_ref[:, pl.ds(slot * BLOCK, BLOCK)] = low
    for p in range(slots // 2):
        one, two = pl.ds(p * PAIR, BLOCK), pl.ds(p * PAIR + BLOCK, BLOCK)
        cross = dot_t(high_ref[:, one], high_ref[:, two]) + (
            dot_t(high_ref[:, one], low_ref[:, two]) + dot_t(low_ref[:, one], high_ref[:, two])
        )
        for j in range(per):
            part_ref[p * per + j] = cross[j * rows:(j + 1) * rows]


def set_generator(total_rows, cross, first, second, kf, kh, kl):
    eye = eye_mask(BLOCK)
    sign = jnp.where(eye, 0.0, jnp.where(upper_mask(BLOCK), 1.0, -1.0))
    scale = 1.0 / total_rows
    roots = []
    for block in (first, second):
        kept = jnp.where(eye, block * scale, 0.0)
        roots.append(
            (
                lax.rsqrt(jnp.sum(kept, axis=1, keepdims=True) + 1e-06),
                lax.rsqrt(jnp.sum(kept, axis=0, keepdims=True) + 1e-06),
            )
        )
    k11 = first * scale * roots[0][0] * roots[0][1] * sign
    k22 = second * scale * roots[1][0] * roots[1][1] * sign
    k12 = cross * scale * roots[0][0] * roots[1][1]
    total = jnp.sum(k11 * k11 + k22 * k22 + 2.0 * (k12 * k12), keepdims=True)
    lo, hi = pl.ds(0, BLOCK), pl.ds(BLOCK, BLOCK)
    for r, c, block in ((lo, lo, k11), (lo, hi, k12), (hi, lo, -k12.T), (hi, hi, k22)):
        kf[r, c] = block
        high, low = split(block)
        kh[r, c] = high
        kl[r, c] = low
    return 1.0 / (1.0 + jnp.sqrt(total))


def rotations(pairs, generator, works, out_high, out_low):
    part = [pl.ds(0, BLOCK), pl.ds(BLOCK, BLOCK)]
    upper = ((0, 0), (0, 1), (1, 1))
    held = [{} for _ in works]

    def turn(p):
        return p if len(works) == pairs else 0

    def start(p):
        c = generator(p, works[turn(p)])
        u = c * c
        b0, b1, b2, b3, b4 = POLY
        held[turn(p)]["c"] = c
        held[turn(p)]["k"] = (
            u,
            b0 + u * (b1 + u * (b2 + u * (b3 + u * b4))),
            b1 + u * (2 * b2 + u * (3 * b3 + u * 4 * b4)),
            b2 + u * (3 * b3 + u * 6 * b4),
            b3 + u * 4 * b4,
            b4,
        )

    def block(ah, al, bh, bl, i, j):
        r, c = part[i], part[j]
        return dot(ah[r, :], bh[:, c]) + (dot(ah[r, :], bl[:, c]) + dot(al[r, :], bh[:, c]))

    def put(high, low, i, j, value):
        high[part[i], part[j]], low[part[i], part[j]] = split(value)

    def put_symmetric(high, low, i, j, value):
        put(high, low, i, j, value)
        if i != j:
            put(high, low, j, i, value.T)

    def square(p):
        kf, kh, kl, sf, sh, sl, vf, vh, vl, th, tl, xh, xl, yh, yl = works[turn(p)]
        for i, j in upper:
            s = -held[turn(p)]["k"][0] * block(kh, kl, kh, kl, i, j)
            sf[part[i], part[j]] = s
            put_symmetric(sh, sl, i, j, s)

    def fourth(p):
        kf, kh, kl, sf, sh, sl, vf, vh, vl, th, tl, xh, xl, yh, yl = works[turn(p)]
        u, a0, a1, a2, a3, a4 = held[turn(p)]["k"]
        for i, j in upper:
            v = block(sh, sl, sh, sl, i, j)
            vf[part[i], part[j]] = v
            put_symmetric(vh, vl, i, j, v)
            put_symmetric(th, tl, i, j, a3 * sf[part[i], part[j]] + a4 * v)

    def polynomial(p):
        kf, kh, kl, sf, sh, sl, vf, vh, vl, th, tl, xh, xl, yh, yl = works[turn(p)]
        u, a0, a1, a2, a3, a4 = held[turn(p)]["k"]
        for i, j in upper:
            t = a1 * sf[part[i], part[j]] + a2 * vf[part[i], part[j]] + block(vh, vl, th, tl, i, j)
            vf[part[i], part[j]] = t
            put_symmetric(sh, sl, i, j, t)

    def second(p):
        kf, kh, kl, sf, sh, sl, vf, vh, vl, th, tl, xh, xl, yh, yl = works[turn(p)]
        u, a0, a1, a2, a3, a4 = held[turn(p)]["k"]
        c = held[turn(p)]["c"]
        for i, j in upper:
            odd = a0 * kf[part[i], part[j]] + block(kh, kl, sh, sl, i, j)
            even = vf[part[i], part[j]]
            if i == j:
                even = jnp.where(eye_mask(BLOCK), even + a0, even)
            x, y = c * (even - odd), c * (even + odd)
            sf[part[i], part[j]] = x
            put(xh, xl, i, j, x)
            put(yh, yl, i, j, y)
            if i != j:
                turned = y.T
                sf[part[j], part[i]] = turned
                put(xh, xl, j, i, turned)
                put(yh, yl, j, i, x.T)

    def metric(p):
        kf, kh, kl, sf, sh, sl, vf, vh, vl, th, tl, xh, xl, yh, yl = works[turn(p)]
        for i, j in upper:
            put_symmetric(vh, vl, i, j, block(yh, yl, xh, xl, i, j))

    def third(p):
        kf, kh, kl, sf, sh, sl, vf, vh, vl, th, tl, xh, xl, yh, yl = works[turn(p)]
        for cols in part:
            r = 1.5 * sf[:, cols] - 0.5 * product(xh, xl, vh, vl, cols)
            out_high[p, :, cols], out_low[p, :, cols] = split(r)

    stages = (start, square, fourth, polynomial, second, metric, third)
    if len(works) == pairs:
        for step in range(len(stages) + pairs - 1):
            for p in range(pairs):
                if 0 <= step - p < len(stages):
                    stages[step - p](p)
    else:

        @pl.loop(0, pairs)
        def _(p):
            for stage in stages:
                stage(p)


def fetch(table_ref, held, sem):
    copy = pltpu.make_async_copy(table_ref, held, sem)
    copy.start()
    return copy


def leave(round_index, slots, src_ref, high_ref, low_ref, rh_ref, rl_ref, right_ref, left_ref):
    for step, out_ref in ((1, right_ref), (-1, left_ref)):
        slot = leaving(src_ref, round_index, step, slots)
        pair, half = slot >> 1, slot & 1
        rows = pl.ds(pl.multiple_of(pair * PAIR, PAIR), PAIR)
        cols = pl.ds(pl.multiple_of(half * BLOCK, BLOCK), BLOCK)
        out_ref[...] = product(
            high_ref.at[:, rows], low_ref.at[:, rows], rh_ref.at[pair], rl_ref.at[pair], cols
        )


def first_rotate(total_rows, slots, table_ref, sum_ref, high_ref, low_ref,
                 right_ref, left_ref, rh_ref, rl_ref, gh_ref, gl_ref, src_ref, sem, *rest):
    table = fetch(table_ref, src_ref, sem)
    rows = (sum_ref.shape[1] - 8) // 2
    per = BLOCK // rows
    works = [rest[at:at + 15] for at in range(0, len(rest), 15)]
    lo, hi = pl.ds(0, BLOCK), pl.ds(BLOCK, BLOCK)

    def generator(p, work):
        first_chunk = 2 * per * p

        def unpack(chunk):
            halves = [sum_ref[pl.ds(chunk, per), pl.ds(at, rows), :].reshape(BLOCK, LANES) for at in (0, rows)]
            return jnp.concatenate(halves, axis=1)

        cross, both = unpack(first_chunk), unpack(first_chunk + per)
        diagonal = jnp.concatenate([sum_ref[first_chunk, pl.ds(2 * rows + at, 1), :] for at in (0, 1)], axis=1)
        turned = both.T
        eye, upper = eye_mask(BLOCK), upper_mask(BLOCK)
        first = jnp.where(eye | upper, both, turned)
        second = jnp.where(eye, diagonal, jnp.where(upper, turned, both))
        for r, c, block in ((lo, lo, first), (lo, hi, cross), (hi, lo, cross.T), (hi, hi, second)):
            high, low = split(block)
            gh_ref[p, r, c] = high
            gl_ref[p, r, c] = low
        return set_generator(total_rows, cross, first, second, *work[:3])

    rotations(slots // 2, generator, works, rh_ref, rl_ref)
    table.wait()
    leave(0, slots, src_ref, high_ref, low_ref, rh_ref, rl_ref, right_ref, left_ref)


def later_rotate(round_index, last, total_rows, slots, table_ref, sum_ref, self_ref,
                 high_ref, low_ref, right_ref, left_ref, rh_ref, rl_ref, *rest):
    rows = sum_ref.shape[1]
    per = BLOCK // rows
    if not last:
        gh_ref, gl_ref = rest[:2]
    src_ref, sem, *rest = rest if last else rest[2:]
    table = fetch(table_ref, src_ref, sem)
    works = [rest[at:at + 15] for at in range(0, len(rest), 15)]
    lo, hi = pl.ds(0, BLOCK), pl.ds(BLOCK, BLOCK)

    def generator(p, work):
        cross = sum_ref[pl.ds(p * per, per)].reshape(BLOCK, BLOCK)
        first, second = self_ref[2 * p], self_ref[2 * p + 1]
        if not last:
            for r, c, block in ((lo, lo, first), (lo, hi, cross), (hi, lo, cross.T), (hi, hi, second)):
                high, low = split(block)
                gh_ref[p, r, c] = high
                gl_ref[p, r, c] = low
        return set_generator(total_rows, cross, first, second, *work[:3])

    rotations(slots // 2, generator, works, rh_ref, rl_ref)
    table.wait()
    leave(round_index, slots, src_ref, high_ref, low_ref, rh_ref, rl_ref, right_ref, left_ref)


def carry_self(round_index, slots, table_ref, gh_ref, gl_ref, rh_ref, rl_ref,
               self_ref, right_ref, left_ref, src_ref, sem, *work):
    table = fetch(table_ref, src_ref, sem)
    @pl.loop(0, slots // 2)
    def _(p):
        for half in range(2):
            cols = pl.ds(half * BLOCK, BLOCK)
            yh, yl = work[2 * half:2 * half + 2]
            yh[...], yl[...] = split(product(gh_ref.at[p], gl_ref.at[p], rh_ref.at[p], rl_ref.at[p], cols))
        for half in range(2):
            cols = pl.ds(half * BLOCK, BLOCK)
            yh, yl = work[2 * half:2 * half + 2]
            self_ref[2 * p + half] = dot_t(rh_ref[p, :, cols], yh[...]) + (
                dot_t(rh_ref[p, :, cols], yl[...]) + dot_t(rl_ref[p, :, cols], yh[...])
            )

    table.wait()
    for step, out_ref in ((1, right_ref), (-1, left_ref)):
        slot = leaving(src_ref, round_index, step, slots)
        out_ref[:LANES, :] = self_ref[slot, :LANES, :]
        for half in range(2):
            rows = pl.ds(LANES + half * LANES // 2, LANES // 2)
            out_ref[LANES:, pl.ds(half * LANES, LANES)] = self_ref[slot, rows, LANES:]


def apply(slots, high_ref, low_ref, rh_ref, rl_ref, after_ref, own_ref):
    @pl.loop(0, slots // 2)
    def _(p):
        rows = pl.ds(pl.multiple_of(p * PAIR, PAIR), PAIR)
        for half in range(2):
            own_ref[2 * p + half] = product(
                high_ref.at[:, rows], low_ref.at[:, rows], rh_ref.at[p], rl_ref.at[p], pl.ds(half * BLOCK, BLOCK)
            )


def apply_last(round_index, slots, table_ref, high_ref, low_ref, rh_ref, rl_ref, out_ref, src_ref, sem, own_ref, sems):
    table = fetch(table_ref, src_ref, sem)

    @pl.loop(0, slots)
    def _(slot):
        pair, half = slot >> 1, slot & 1
        rows = pl.ds(pl.multiple_of(pair * PAIR, PAIR), PAIR)
        cols = pl.ds(pl.multiple_of(half * BLOCK, BLOCK), BLOCK)
        own_ref[slot] = product(high_ref.at[:, rows], low_ref.at[:, rows], rh_ref.at[pair], rl_ref.at[pair], cols)

    table.wait()
    offsets = [own_source(src_ref, round_index, slot, slots) for slot in range(slots)]
    for wait in (False, True):
        for slot, offset in enumerate(offsets):
            @pl.when((offset >= 0) & (offset < slots))
            def _():
                kept = own_ref.at[jnp.clip(offset, 0, slots - 1)]
                goal = out_ref.at[:, pl.ds(slot * BLOCK, BLOCK)]
                copy = pltpu.make_async_copy(kept, goal, sems.at[slot])
                copy.wait() if wait else copy.start()


def settle(round_index, slots, src_ref, most_ref, lower_ref, upper_ref, out_ref, sems):
    offsets = own_sources(src_ref, round_index, slots)
    for wait in (False, True):
        for slot, offset in enumerate(offsets):
            goal = out_ref.at[:, pl.ds(slot * BLOCK, BLOCK)]

            @pl.when(offset < 0)
            def _():
                copy = pltpu.make_async_copy(lower_ref, goal, sems.at[slot])
                copy.wait() if wait else copy.start()

            @pl.when(offset >= slots)
            def _():
                copy = pltpu.make_async_copy(upper_ref, goal, sems.at[slot])
                copy.wait() if wait else copy.start()


def to_next(x, by):
    count = lax.axis_size("pair")
    return lax.ppermute(x, "pair", [(i, (i + by) % count) for i in range(count)])


def add_up(pieces_ref, out_ref):
    total = jnp.sum(pieces_ref[...], axis=0)

    @pl.loop(0, out_ref.shape[0])
    def _(chunk):
        out_ref[chunk] = total


def add_up_and_take(round_index, slots, table_ref, pieces_ref, self_ref, lower_ref, upper_ref,
                    out_ref, taken_ref, lower_full, upper_full):
    add_up(pieces_ref, out_ref)
    for packed, full in ((lower_ref, lower_full), (upper_ref, upper_full)):
        full[:LANES, :] = packed[:LANES, :]
        full[LANES:, :LANES] = packed[:LANES, LANES:].T
        for half in range(2):
            rows = pl.ds(LANES + half * LANES // 2, LANES // 2)
            full[rows, LANES:] = packed[LANES:, pl.ds(half * LANES, LANES)]
    for slot, offset in enumerate(own_sources(table_ref, round_index, slots)):
        taken_ref[slot] = picked(offset, slots, self_ref, lower_full, upper_full)


def from_rows(part):
    return lax.all_to_all(part, "row", 0, 0, tiled=True)


def body(matrix, sources):
    rows, columns = matrix.shape
    slots = columns // BLOCK
    pairs = slots // 2
    row_count = lax.axis_size("row")
    total_rows = rows * row_count
    f32 = partial(jax.ShapeDtypeStruct, dtype=F32)
    bf16 = partial(jax.ShapeDtypeStruct, dtype=BF16)
    square = (PAIR, PAIR)
    f, h = pltpu.VMEM(square, F32), pltpu.VMEM(square, BF16)
    work = [f, h, h, f, h, h, f, h, h, h, h, h, h, h, h]
    product_flops = 2 * PAIR**3 * 3
    sems = pltpu.SemaphoreType.DMA((slots,))
    part, high, low = call(
        first_gram,
        (f32((row_count, BLOCK // LANES * slots * BLOCK // row_count + 8, LANES)), bf16(matrix.shape), bf16(matrix.shape)),
        [VMEM],
        flops=3 * pairs * product_flops // 4,
    )(matrix)
    part, sources = lax.optimization_barrier((part, sources))
    block, small = f32((rows, BLOCK)), f32((BLOCK * 3 // 4, BLOCK))
    table = [pltpu.SMEM(sources.shape, jnp.int32), pltpu.SemaphoreType.DMA]
    carried = ()
    summed = from_rows(call(add_up, f32(part.shape), [VMEM])(from_rows(part)))
    for index in range(ROUNDS):
        last = index == ROUNDS - 1
        kernel = first_rotate if index == 0 else partial(later_rotate, index, last)
        right, left, rh, rl, *gram = call(
            partial(kernel, total_rows, slots),
            (block, block) + (bf16((pairs,) + square),) * (2 if last else 4),
            [ANY] + [VMEM] * (3 + len(carried)),
            table + work * (pairs if index in UNROLLED else 1),
            flops=7 * pairs * product_flops,
            mib=20,
        )(sources, summed, *carried, high, low)
        lower, upper = to_next(right, 1), to_next(left, -1)
        if last:
            most = call(
                partial(apply_last, index, slots),
                f32(matrix.shape),
                [ANY] + [VMEM] * 4,
                table + [pltpu.VMEM((slots, rows, BLOCK), F32), sems],
                flops=pairs * product_flops,
                out_spec=ANY,
            )(sources, high, low, rh, rl)
            return call(
                partial(settle, index, slots),
                f32(matrix.shape),
                [VMEM, ANY, VMEM, VMEM],
                [sems],
                out_spec=ANY,
                alias={1: 0},
            )(sources, most, lower, upper)
        selves, self_right, self_left = call(
            partial(carry_self, index, slots),
            (f32((slots, BLOCK, BLOCK)), small, small),
            [ANY] + [VMEM] * 4,
            table + [pltpu.VMEM((PAIR, BLOCK), BF16)] * 4,
            flops=3 * pairs * product_flops // 2,
        )(sources, *gram, rh, rl)
        own = call(
            partial(apply, slots),
            f32((slots, rows, BLOCK)),
            [VMEM] * 4 + [ANY],
            flops=pairs * product_flops,
        )(high, low, rh, rl, selves)
        lower_self, upper_self = to_next(self_right, 1), to_next(self_left, -1)
        part, high, low = call(
            partial(cross_gram, index, slots),
            (f32((row_count, pairs * BLOCK // row_count, BLOCK)), bf16(matrix.shape), bf16(matrix.shape)),
            [VMEM] * 4,
            flops=pairs * product_flops // 4,
        )(sources, own, lower, upper)
        part, lower_self, upper_self = lax.optimization_barrier((part, lower_self, upper_self))
        mine, selves = call(
            partial(add_up_and_take, index, slots),
            (f32(part.shape), f32((slots, BLOCK, BLOCK))),
            [VMEM] * 5,
            [pltpu.VMEM((BLOCK, BLOCK), F32)] * 2,
        )(sources, from_rows(part), selves, lower_self, upper_self)
        carried = (selves,)
        summed = from_rows(mine)


def solution(mesh):
    placed = (P("row", "pair"), P())
    return jax.shard_map(
        body, mesh=mesh, in_specs=placed, out_specs=P("row", "pair"), check_vma=False
    )
```

```python
from functools import partial

import jax
import jax.numpy as jnp
from jax import lax
from jax.experimental import pallas as pl
from jax.experimental.pallas import tpu as pltpu
from jax.sharding import PartitionSpec as P

BLOCK = 256
PAIR = 2 * BLOCK
LANES = 128
ROUNDS = 3
UNROLLED = (0, 1, 2)
F32 = jnp.float32
BF16 = jnp.bfloat16
POLY = (2.25, -2.4375, 1.6875, -0.5625, 0.0625)

VMEM = pl.BlockSpec(memory_space=pltpu.VMEM)
ANY = pl.BlockSpec(memory_space=pl.ANY)


def call(kernel, out_shape, in_specs, scratch=(), flops=0, mib=10, out_spec=VMEM, alias=None):
    return pl.pallas_call(
        kernel,
        out_shape=out_shape,
        in_specs=in_specs,
        out_specs=jax.tree.map(lambda _: out_spec, out_shape),
        scratch_shapes=list(scratch),
        input_output_aliases=alias or {},
        compiler_params=pltpu.CompilerParams(vmem_limit_bytes=mib * 1024 * 1024),
        cost_estimate=pl.CostEstimate(flops=flops, bytes_accessed=4_000_000, transcendentals=0),
    )


def split(x):
    high = x.astype(BF16)
    return high, (x - high.astype(F32)).astype(BF16)


def dot(a, b):
    return jnp.dot(a, b, preferred_element_type=F32)


def dot_t(a, b):
    return lax.dot_general(a, b, (((0,), (0,)), ((), ())), preferred_element_type=F32)


def product(ah, al, bh, bl, cols, mul=dot):
    return mul(ah[...], bh[:, cols]) + (mul(ah[...], bl[:, cols]) + mul(al[...], bh[:, cols]))


def eye_mask(n):
    return lax.broadcasted_iota(jnp.int32, (n, n), 0) == lax.broadcasted_iota(jnp.int32, (n, n), 1)


def upper_mask(n):
    return lax.broadcasted_iota(jnp.int32, (n, n), 0) < lax.broadcasted_iota(jnp.int32, (n, n), 1)


def own_source(src_ref, round_index, slot, slots):
    base = lax.axis_index("pair") * slots
    return src_ref[round_index, base + slot] - base


def own_sources(table_ref, round_index, slots):
    base = lax.axis_index("pair") * slots
    row = table_ref[pl.ds(round_index, 1), :].astype(F32)
    lane = lax.broadcasted_iota(jnp.int32, row.shape, 1)
    return [jnp.sum(jnp.where(lane == base + slot, row, 0.0)).astype(jnp.int32) - base for slot in range(slots)]


def leaving(src_ref, round_index, step, slots):
    base = lax.axis_index("pair") * slots
    last = src_ref.shape[1] - slots
    there = jnp.clip(base + step * slots, 0, last)
    found = jnp.int32(0)
    for slot in range(slots):
        offset = src_ref[round_index, there + slot] - base
        found = jnp.where((offset >= 0) & (offset < slots), offset, found)
    return found


def picked(offset, slots, own_ref, lower_ref, upper_ref):
    own = own_ref[jnp.clip(offset, 0, slots - 1)]
    return jnp.where(offset < 0, lower_ref[...], jnp.where(offset >= slots, upper_ref[...], own))


def first_gram(a_ref, part_ref, high_ref, low_ref):
    pairs = a_ref.shape[1] // PAIR
    rows = (part_ref.shape[1] - 8) // 2
    per = BLOCK // rows
    part_ref[:, 2 * rows:, :] = jnp.zeros((part_ref.shape[0], 8, LANES), F32)
    for p in range(pairs):
        one, two = pl.ds(p * PAIR, BLOCK), pl.ds(p * PAIR + BLOCK, BLOCK)
        for cols in (one, two):
            high_ref[:, cols], low_ref[:, cols] = split(a_ref[:, cols])

        def gram(x, y):
            return dot_t(high_ref[:, x], high_ref[:, y]) + (
                dot_t(high_ref[:, x], low_ref[:, y]) + dot_t(low_ref[:, x], high_ref[:, y])
            )

        cross = gram(one, two)
        first = gram(one, one)
        second = gram(two, two)
        eye = eye_mask(BLOCK)
        diagonal = jnp.sum(jnp.where(eye, second, 0.0), axis=0, keepdims=True)
        both = jnp.where(eye | upper_mask(BLOCK), first, second)
        start = 2 * per * p
        for first_chunk, block in ((start, cross), (start + per, both)):
            for j in range(per):
                piece = block[j * rows:(j + 1) * rows]
                part_ref[first_chunk + j, :rows, :] = piece[:, :LANES]
                part_ref[first_chunk + j, rows:2 * rows, :] = piece[:, LANES:]
        part_ref[start, 2 * rows:2 * rows + 1, :] = diagonal[:, :LANES]
        part_ref[start, 2 * rows + 1:2 * rows + 2, :] = diagonal[:, LANES:]


def cross_gram(round_index, slots, src_ref, own_ref, lower_ref, upper_ref, part_ref, high_ref, low_ref):
    rows = part_ref.shape[1]
    per = BLOCK // rows
    for slot, offset in enumerate(own_sources(src_ref, round_index, slots)):
        high, low = split(picked(offset, slots, own_ref, lower_ref, upper_ref))
        high_ref[:, pl.ds(slot * BLOCK, BLOCK)] = high
        low_ref[:, pl.ds(slot * BLOCK, BLOCK)] = low
    for p in range(slots // 2):
        one, two = pl.ds(p * PAIR, BLOCK), pl.ds(p * PAIR + BLOCK, BLOCK)
        cross = dot_t(high_ref[:, one], high_ref[:, two]) + (
            dot_t(high_ref[:, one], low_ref[:, two]) + dot_t(low_ref[:, one], high_ref[:, two])
        )
        for j in range(per):
            part_ref[p * per + j] = cross[j * rows:(j + 1) * rows]


def set_generator(total_rows, cross, first, second, kf, kh, kl):
    eye = eye_mask(BLOCK)
    sign = jnp.where(eye, 0.0, jnp.where(upper_mask(BLOCK), 1.0, -1.0))
    scale = 1.0 / total_rows
    roots = []
    for block in (first, second):
        kept = jnp.where(eye, block * scale, 0.0)
        roots.append(
            (
                lax.rsqrt(jnp.sum(kept, axis=1, keepdims=True) + 1e-06),
                lax.rsqrt(jnp.sum(kept, axis=0, keepdims=True) + 1e-06),
            )
        )
    k11 = first * scale * roots[0][0] * roots[0][1] * sign
    k22 = second * scale * roots[1][0] * roots[1][1] * sign
    k12 = cross * scale * roots[0][0] * roots[1][1]
    total = jnp.sum(k11 * k11 + k22 * k22 + 2.0 * (k12 * k12), keepdims=True)
    lo, hi = pl.ds(0, BLOCK), pl.ds(BLOCK, BLOCK)
    for r, c, block in ((lo, lo, k11), (lo, hi, k12), (hi, lo, -k12.T), (hi, hi, k22)):
        kf[r, c] = block
        high, low = split(block)
        kh[r, c] = high
        kl[r, c] = low
    return 1.0 / (1.0 + jnp.sqrt(total))


def rotations(pairs, generator, works, out_high, out_low):
    part = [pl.ds(0, BLOCK), pl.ds(BLOCK, BLOCK)]
    upper = ((0, 0), (0, 1), (1, 1))
    held = [{} for _ in works]

    def turn(p):
        return p if len(works) == pairs else 0

    def start(p):
        c = generator(p, works[turn(p)])
        u = c * c
        b0, b1, b2, b3, b4 = POLY
        held[turn(p)]["c"] = c
        held[turn(p)]["k"] = (
            u,
            b0 + u * (b1 + u * (b2 + u * (b3 + u * b4))),
            b1 + u * (2 * b2 + u * (3 * b3 + u * 4 * b4)),
            b2 + u * (3 * b3 + u * 6 * b4),
            b3 + u * 4 * b4,
            b4,
        )

    def block(ah, al, bh, bl, i, j):
        r, c = part[i], part[j]
        return dot(ah[r, :], bh[:, c]) + (dot(ah[r, :], bl[:, c]) + dot(al[r, :], bh[:, c]))

    def put(high, low, i, j, value):
        high[part[i], part[j]], low[part[i], part[j]] = split(value)

    def put_symmetric(high, low, i, j, value):
        put(high, low, i, j, value)
        if i != j:
            put(high, low, j, i, value.T)

    def square(p):
        kf, kh, kl, sf, sh, sl, vf, vh, vl, th, tl, xh, xl, yh, yl = works[turn(p)]
        for i, j in upper:
            s = -held[turn(p)]["k"][0] * block(kh, kl, kh, kl, i, j)
            sf[part[i], part[j]] = s
            put_symmetric(sh, sl, i, j, s)

    def fourth(p):
        kf, kh, kl, sf, sh, sl, vf, vh, vl, th, tl, xh, xl, yh, yl = works[turn(p)]
        u, a0, a1, a2, a3, a4 = held[turn(p)]["k"]
        for i, j in upper:
            v = block(sh, sl, sh, sl, i, j)
            vf[part[i], part[j]] = v
            put_symmetric(vh, vl, i, j, v)
            put_symmetric(th, tl, i, j, a3 * sf[part[i], part[j]] + a4 * v)

    def polynomial(p):
        kf, kh, kl, sf, sh, sl, vf, vh, vl, th, tl, xh, xl, yh, yl = works[turn(p)]
        u, a0, a1, a2, a3, a4 = held[turn(p)]["k"]
        for i, j in upper:
            t = a1 * sf[part[i], part[j]] + a2 * vf[part[i], part[j]] + block(vh, vl, th, tl, i, j)
            vf[part[i], part[j]] = t
            put_symmetric(sh, sl, i, j, t)

    def second(p):
        kf, kh, kl, sf, sh, sl, vf, vh, vl, th, tl, xh, xl, yh, yl = works[turn(p)]
        u, a0, a1, a2, a3, a4 = held[turn(p)]["k"]
        c = held[turn(p)]["c"]
        for i, j in upper:
            odd = a0 * kf[part[i], part[j]] + block(kh, kl, sh, sl, i, j)
            even = vf[part[i], part[j]]
            if i == j:
                even = jnp.where(eye_mask(BLOCK), even + a0, even)
            x, y = c * (even - odd), c * (even + odd)
            sf[part[i], part[j]] = x
            put(xh, xl, i, j, x)
            put(yh, yl, i, j, y)
            if i != j:
                turned = y.T
                sf[part[j], part[i]] = turned
                put(xh, xl, j, i, turned)
                put(yh, yl, j, i, x.T)

    def metric(p):
        kf, kh, kl, sf, sh, sl, vf, vh, vl, th, tl, xh, xl, yh, yl = works[turn(p)]
        for i, j in upper:
            put_symmetric(vh, vl, i, j, block(yh, yl, xh, xl, i, j))

    def third(p):
        kf, kh, kl, sf, sh, sl, vf, vh, vl, th, tl, xh, xl, yh, yl = works[turn(p)]
        for cols in part:
            r = 1.5 * sf[:, cols] - 0.5 * product(xh, xl, vh, vl, cols)
            out_high[p, :, cols], out_low[p, :, cols] = split(r)

    stages = (start, square, fourth, polynomial, second, metric, third)
    if len(works) == pairs:
        for step in range(len(stages) + pairs - 1):
            for p in range(pairs):
                if 0 <= step - p < len(stages):
                    stages[step - p](p)
    else:

        @pl.loop(0, pairs)
        def _(p):
            for stage in stages:
                stage(p)


def fetch(table_ref, held, sem):
    copy = pltpu.make_async_copy(table_ref, held, sem)
    copy.start()
    return copy


def leave(round_index, slots, src_ref, high_ref, low_ref, rh_ref, rl_ref, right_ref, left_ref):
    for step, out_ref in ((1, right_ref), (-1, left_ref)):
        slot = leaving(src_ref, round_index, step, slots)
        pair, half = slot >> 1, slot & 1
        rows = pl.ds(pl.multiple_of(pair * PAIR, PAIR), PAIR)
        cols = pl.ds(pl.multiple_of(half * BLOCK, BLOCK), BLOCK)
        out_ref[...] = product(
            high_ref.at[:, rows], low_ref.at[:, rows], rh_ref.at[pair], rl_ref.at[pair], cols
        )


def first_rotate(total_rows, slots, table_ref, sum_ref, high_ref, low_ref,
                 right_ref, left_ref, rh_ref, rl_ref, gh_ref, gl_ref, src_ref, sem, *rest):
    table = fetch(table_ref, src_ref, sem)
    rows = (sum_ref.shape[1] - 8) // 2
    per = BLOCK // rows
    works = [rest[at:at + 15] for at in range(0, len(rest), 15)]
    lo, hi = pl.ds(0, BLOCK), pl.ds(BLOCK, BLOCK)

    def generator(p, work):
        first_chunk = 2 * per * p

        def unpack(chunk):
            halves = [sum_ref[pl.ds(chunk, per), pl.ds(at, rows), :].reshape(BLOCK, LANES) for at in (0, rows)]
            return jnp.concatenate(halves, axis=1)

        cross, both = unpack(first_chunk), unpack(first_chunk + per)
        diagonal = jnp.concatenate([sum_ref[first_chunk, pl.ds(2 * rows + at, 1), :] for at in (0, 1)], axis=1)
        turned = both.T
        eye, upper = eye_mask(BLOCK), upper_mask(BLOCK)
        first = jnp.where(eye | upper, both, turned)
        second = jnp.where(eye, diagonal, jnp.where(upper, turned, both))
        for r, c, block in ((lo, lo, first), (lo, hi, cross), (hi, lo, cross.T), (hi, hi, second)):
            high, low = split(block)
            gh_ref[p, r, c] = high
            gl_ref[p, r, c] = low
        return set_generator(total_rows, cross, first, second, *work[:3])

    rotations(slots // 2, generator, works, rh_ref, rl_ref)
    table.wait()
    leave(0, slots, src_ref, high_ref, low_ref, rh_ref, rl_ref, right_ref, left_ref)


def later_rotate(round_index, last, total_rows, slots, table_ref, sum_ref, self_ref,
                 high_ref, low_ref, right_ref, left_ref, rh_ref, rl_ref, *rest):
    rows = sum_ref.shape[1]
    per = BLOCK // rows
    if not last:
        gh_ref, gl_ref = rest[:2]
    src_ref, sem, *rest = rest if last else rest[2:]
    table = fetch(table_ref, src_ref, sem)
    works = [rest[at:at + 15] for at in range(0, len(rest), 15)]
    lo, hi = pl.ds(0, BLOCK), pl.ds(BLOCK, BLOCK)

    def generator(p, work):
        cross = sum_ref[pl.ds(p * per, per)].reshape(BLOCK, BLOCK)
        first, second = self_ref[2 * p], self_ref[2 * p + 1]
        if not last:
            for r, c, block in ((lo, lo, first), (lo, hi, cross), (hi, lo, cross.T), (hi, hi, second)):
                high, low = split(block)
                gh_ref[p, r, c] = high
                gl_ref[p, r, c] = low
        return set_generator(total_rows, cross, first, second, *work[:3])

    rotations(slots // 2, generator, works, rh_ref, rl_ref)
    table.wait()
    leave(round_index, slots, src_ref, high_ref, low_ref, rh_ref, rl_ref, right_ref, left_ref)


def carry_self(round_index, slots, table_ref, gh_ref, gl_ref, rh_ref, rl_ref,
               self_ref, right_ref, left_ref, src_ref, sem, *work):
    table = fetch(table_ref, src_ref, sem)
    @pl.loop(0, slots // 2)
    def _(p):
        for half in range(2):
            cols = pl.ds(half * BLOCK, BLOCK)
            yh, yl = work[2 * half:2 * half + 2]
            yh[...], yl[...] = split(product(gh_ref.at[p], gl_ref.at[p], rh_ref.at[p], rl_ref.at[p], cols))
        for half in range(2):
            cols = pl.ds(half * BLOCK, BLOCK)
            yh, yl = work[2 * half:2 * half + 2]
            self_ref[2 * p + half] = dot_t(rh_ref[p, :, cols], yh[...]) + (
                dot_t(rh_ref[p, :, cols], yl[...]) + dot_t(rl_ref[p, :, cols], yh[...])
            )

    table.wait()
    for step, out_ref in ((1, right_ref), (-1, left_ref)):
        slot = leaving(src_ref, round_index, step, slots)
        out_ref[:LANES, :] = self_ref[slot, :LANES, :]
        for half in range(2):
            rows = pl.ds(LANES + half * LANES // 2, LANES // 2)
            out_ref[LANES:, pl.ds(half * LANES, LANES)] = self_ref[slot, rows, LANES:]


def apply(slots, high_ref, low_ref, rh_ref, rl_ref, after_ref, own_ref):
    @pl.loop(0, slots // 2)
    def _(p):
        rows = pl.ds(pl.multiple_of(p * PAIR, PAIR), PAIR)
        for half in range(2):
            own_ref[2 * p + half] = product(
                high_ref.at[:, rows], low_ref.at[:, rows], rh_ref.at[p], rl_ref.at[p], pl.ds(half * BLOCK, BLOCK)
            )


def apply_last(round_index, slots, table_ref, high_ref, low_ref, rh_ref, rl_ref, out_ref, src_ref, sem, own_ref, sems):
    table = fetch(table_ref, src_ref, sem)

    @pl.loop(0, slots)
    def _(slot):
        pair, half = slot >> 1, slot & 1
        rows = pl.ds(pl.multiple_of(pair * PAIR, PAIR), PAIR)
        cols = pl.ds(pl.multiple_of(half * BLOCK, BLOCK), BLOCK)
        own_ref[slot] = product(high_ref.at[:, rows], low_ref.at[:, rows], rh_ref.at[pair], rl_ref.at[pair], cols)

    table.wait()
    offsets = [own_source(src_ref, round_index, slot, slots) for slot in range(slots)]
    for wait in (False, True):
        for slot, offset in enumerate(offsets):
            @pl.when((offset >= 0) & (offset < slots))
            def _():
                kept = own_ref.at[jnp.clip(offset, 0, slots - 1)]
                goal = out_ref.at[:, pl.ds(slot * BLOCK, BLOCK)]
                copy = pltpu.make_async_copy(kept, goal, sems.at[slot])
                copy.wait() if wait else copy.start()


def settle(round_index, slots, src_ref, most_ref, lower_ref, upper_ref, out_ref, sems):
    offsets = own_sources(src_ref, round_index, slots)
    for wait in (False, True):
        for slot, offset in enumerate(offsets):
            goal = out_ref.at[:, pl.ds(slot * BLOCK, BLOCK)]

            @pl.when(offset < 0)
            def _():
                copy = pltpu.make_async_copy(lower_ref, goal, sems.at[slot])
                copy.wait() if wait else copy.start()

            @pl.when(offset >= slots)
            def _():
                copy = pltpu.make_async_copy(upper_ref, goal, sems.at[slot])
                copy.wait() if wait else copy.start()


def to_next(x, by):
    count = lax.axis_size("pair")
    return lax.ppermute(x, "pair", [(i, (i + by) % count) for i in range(count)])


def add_up(pieces_ref, out_ref):
    total = jnp.sum(pieces_ref[...], axis=0)

    @pl.loop(0, out_ref.shape[0], unroll=4)
    def _(chunk):
        out_ref[chunk] = total


def add_up_and_take(round_index, slots, table_ref, pieces_ref, self_ref, lower_ref, upper_ref,
                    out_ref, taken_ref, lower_full, upper_full):
    add_up(pieces_ref, out_ref)
    for packed, full in ((lower_ref, lower_full), (upper_ref, upper_full)):
        full[:LANES, :] = packed[:LANES, :]
        full[LANES:, :LANES] = packed[:LANES, LANES:].T
        for half in range(2):
            rows = pl.ds(LANES + half * LANES // 2, LANES // 2)
            full[rows, LANES:] = packed[LANES:, pl.ds(half * LANES, LANES)]
    for slot, offset in enumerate(own_sources(table_ref, round_index, slots)):
        taken_ref[slot] = picked(offset, slots, self_ref, lower_full, upper_full)


def from_rows(part):
    return lax.all_to_all(part, "row", 0, 0, tiled=True)


def body(matrix, sources):
    rows, columns = matrix.shape
    slots = columns // BLOCK
    pairs = slots // 2
    row_count = lax.axis_size("row")
    total_rows = rows * row_count
    f32 = partial(jax.ShapeDtypeStruct, dtype=F32)
    bf16 = partial(jax.ShapeDtypeStruct, dtype=BF16)
    square = (PAIR, PAIR)
    f, h = pltpu.VMEM(square, F32), pltpu.VMEM(square, BF16)
    work = [f, h, h, f, h, h, f, h, h, h, h, h, h, h, h]
    product_flops = 2 * PAIR**3 * 3
    sems = pltpu.SemaphoreType.DMA((slots,))
    part, high, low = call(
        first_gram,
        (f32((row_count, BLOCK // LANES * slots * BLOCK // row_count + 8, LANES)), bf16(matrix.shape), bf16(matrix.shape)),
        [VMEM],
        flops=3 * pairs * product_flops // 4,
    )(matrix)
    part, sources = lax.optimization_barrier((part, sources))
    block, small = f32((rows, BLOCK)), f32((BLOCK * 3 // 4, BLOCK))
    table = [pltpu.SMEM(sources.shape, jnp.int32), pltpu.SemaphoreType.DMA]
    carried = ()
    summed = from_rows(call(add_up, f32(part.shape), [VMEM])(from_rows(part)))
    for index in range(ROUNDS):
        last = index == ROUNDS - 1
        kernel = first_rotate if index == 0 else partial(later_rotate, index, last)
        right, left, rh, rl, *gram = call(
            partial(kernel, total_rows, slots),
            (block, block) + (bf16((pairs,) + square),) * (2 if last else 4),
            [ANY] + [VMEM] * (3 + len(carried)),
            table + work * (pairs if index in UNROLLED else 1),
            flops=7 * pairs * product_flops,
            mib=20,
        )(sources, summed, *carried, high, low)
        lower, upper = to_next(right, 1), to_next(left, -1)
        if last:
            most = call(
                partial(apply_last, index, slots),
                f32(matrix.shape),
                [ANY] + [VMEM] * 4,
                table + [pltpu.VMEM((slots, rows, BLOCK), F32), sems],
                flops=pairs * product_flops,
                out_spec=ANY,
            )(sources, high, low, rh, rl)
            return call(
                partial(settle, index, slots),
                f32(matrix.shape),
                [VMEM, ANY, VMEM, VMEM],
                [sems],
                out_spec=ANY,
                alias={1: 0},
            )(sources, most, lower, upper)
        selves, self_right, self_left = call(
            partial(carry_self, index, slots),
            (f32((slots, BLOCK, BLOCK)), small, small),
            [ANY] + [VMEM] * 4,
            table + [pltpu.VMEM((PAIR, BLOCK), BF16)] * 4,
            flops=3 * pairs * product_flops // 2,
        )(sources, *gram, rh, rl)
        own = call(
            partial(apply, slots),
            f32((slots, rows, BLOCK)),
            [VMEM] * 4 + [ANY],
            flops=pairs * product_flops,
        )(high, low, rh, rl, selves)
        lower_self, upper_self = to_next(self_right, 1), to_next(self_left, -1)
        part, high, low = call(
            partial(cross_gram, index, slots),
            (f32((row_count, pairs * BLOCK // row_count, BLOCK)), bf16(matrix.shape), bf16(matrix.shape)),
            [VMEM] * 4,
            flops=pairs * product_flops // 4,
        )(sources, own, lower, upper)
        part, lower_self, upper_self = lax.optimization_barrier((part, lower_self, upper_self))
        mine, selves = call(
            partial(add_up_and_take, index, slots),
            (f32(part.shape), f32((slots, BLOCK, BLOCK))),
            [VMEM] * 5,
            [pltpu.VMEM((BLOCK, BLOCK), F32)] * 2,
        )(sources, from_rows(part), selves, lower_self, upper_self)
        carried = (selves,)
        summed = from_rows(mine)


def solution(mesh):
    placed = (P("row", "pair"), P())
    return jax.shard_map(
        body, mesh=mesh, in_specs=placed, out_specs=P("row", "pair"), check_vma=False
    )
```
